128 devices in a mesh: dp: 8 (over x, y_lo), pp: 8 (over y_hi, z), tp: 2 (over core).
Axes of the slice: x: 4, y: 4 (y_hi: 2, y_lo: 2; y = y_hi * 2 + y_lo), z: 4, core: 2. Of those that a mesh axis runs over, the one named last changes fastest.
Arguments:
- hidden_in: bfloat16 [8, 4096, 8192], P('pp', 'dp'), may hold values from -6 to 6
- queries: bfloat16 [8, 4096, 4096], P('pp', 'dp', 'tp'), may hold values from -300 to 300
- out_grad: bfloat16 [8, 4096, 4096], P('pp', 'dp', 'tp'), may hold values from -6 to 6
- key_weight: bfloat16 [8, 8192, 512], P('pp', 'dp', 'tp'), may hold values from -0.0625 to 0.0625
- value_weight: bfloat16 [8, 8192, 512], P('pp', 'dp', 'tp'), may hold values from -0.0625 to 0.0625
- doc_lengths: int32 [8, 8, 8], P('pp', 'dp'), may hold values from 1 to 96, 512 in all within a row
Outputs:
- query_grad: bfloat16 [8, 4096, 4096], P('pp', 'dp', 'tp')
- input_grad: bfloat16 [8, 4096, 8192], P('pp', 'dp', 'tp')
- key_weight_grad: float32 [8, 8192, 512], P('pp', 'dp', 'tp')
- value_weight_grad: float32 [8, 8192, 512], P('pp', 'dp', 'tp')
The draws below stay inside these ranges and needn't reach their ends.
Inputs may be any that keep to these rules, and one draw needn't show every extreme that they name: `doc_lengths`: in every section and relay the 8 lengths fill the 512 rows; in every sequence some document has exactly 96 rows.
All inputs are finite; a program needn't handle non-finite values.
Results may differ from the reference program's by a relative error of at most 0.034.
The reference program's roundings to bfloat16 on the way count: a program that leaves them out, or rounds other values in their place, can miss the bound.
Values may be sent and summed in bfloat16 or wider, within the bound.
A program may use at most 128 MiB of HBM per device.

```python
import math
import jax
import jax.numpy as jnp
import numpy as np
from jax import lax

D = 8192
HEADS = 32
KV = 4
HD = 128
S = 512
SECTIONS = 8
PIPES = 8
NDOC = 8
CAP = 96
TOKENS = 4096
N_TP = 2


def draw_queries(key, part):
    key = jax.random.fold_in(key, 11)
    base_key = jax.random.fold_in(key, 0)
    drawn = jax.random.normal(base_key, (SECTIONS, TOKENS, HEADS * HD), jnp.float32)
    drawn = jnp.clip(drawn, -6.0, 6.0)
    return drawn.astype(jnp.bfloat16)


def shard_levels(stream_key, shape, pieces, least, top_value):
    gain, own = 1.0, jax.random.fold_in(stream_key, 6)
    for dim, shards_of in pieces:
        heights = jnp.exp(jax.random.uniform(jax.random.fold_in(own, dim), (shards_of,), jnp.float32, least / len(pieces), top_value / len(pieces)))
        gain = gain * jnp.repeat(heights, shape[dim] // shards_of).reshape([-1 if axis == dim else 1 for axis in range(len(shape))])
    return gain


def profile(count, total, limit, slope):
    loads = [(1 << 20) // math.isqrt(rank ** slope) + 1 for rank in range(2, count + 1)]
    rest, holding = total - limit - (count - 1), [1] * (count - 1)
    while rest > 0:
        candidates = [i for i in range(count - 1) if holding[i] < limit]
        pool, remaining = sum([loads[i] for i in candidates]), rest
        for i in candidates:
            addition = min(limit - holding[i], max(1, remaining * loads[i] // pool), rest)
            holding[i] = holding[i] + addition
            rest = rest - addition
    return np.array([limit] + holding)


def ragged(rng, count, total, bound, slope):
    if count == 2:
        one = jax.random.randint(rng, (), max(1, total - bound), min(bound, total - 1) + 1)
        return jnp.stack([one, total - one])
    sizes = jnp.asarray(profile(count, total, bound, slope), jnp.int32)
    couples = (count - 1) // 2
    source_of, sink = sizes[1:1 + 2 * couples:2], sizes[2:2 + 2 * couples:2]
    slack = jnp.minimum(source_of - 1, bound - sink)
    moved = jax.random.randint(jax.random.fold_in(rng, 1), (couples,), 0, 1 << 20) % (slack + 1)
    sizes = sizes.at[1:1 + 2 * couples:2].set(source_of - moved).at[2:2 + 2 * couples:2].set(sink + moved)
    return sizes[jax.random.permutation(jax.random.fold_in(rng, 2), count)]


def normal_values(rng, dims, deviation, limit, pieces=(), kind=jnp.bfloat16):
    loudness = shard_levels(rng, dims, pieces, -0.22, 0.18) if pieces else 1.0
    values = jax.random.normal(rng, dims, jnp.float32) * deviation * loudness
    return jnp.minimum(jnp.maximum(values, -limit), limit).astype(kind)


def setup_inputs(seed: int = 0) -> dict:
    splits = jax.random.split(jax.random.key(seed), 7)
    return {
        "hidden_in": normal_values(splits[0], (SECTIONS, TOKENS, D), 1.0, 6.0, ((0, 8), (1, 8))),
        "queries": draw_queries(jax.random.fold_in(splits[6], 71), 0),
        "out_grad": normal_values(splits[2], (SECTIONS, TOKENS, HEADS * HD), 1.0, 6.0, ((0, 8), (1, 8), (2, 2))),
        "key_weight": normal_values(splits[3], (SECTIONS, D, KV * HD), D ** -0.5, 0.0625, ((0, 8), (1, 8), (2, 2))),
        "value_weight": normal_values(splits[4], (SECTIONS, D, KV * HD), D ** -0.5, 0.0625, ((0, 8), (1, 8), (2, 2))),
        "doc_lengths": jax.vmap(lambda own: ragged(own, NDOC, S, CAP, 2))(jax.random.split(splits[5], SECTIONS * PIPES)).reshape((SECTIONS, PIPES, NDOC)).astype(jnp.int32),
    }


def attend(query_in, grad_in, key_in, value_in, allowed):
    score_scale = HD ** -0.5
    scores = jnp.einsum("bqkge,bpke->bkgqp", query_in, key_in) * score_scale
    scores = jnp.where(allowed[:, None, None], scores, -1e30)
    row_top = jnp.max(scores, axis=-1, keepdims=True)
    raised = jnp.exp(scores - row_top)
    attn_probs = raised / jnp.sum(raised, axis=-1, keepdims=True)
    probs_low = lax.optimization_barrier(attn_probs.astype(jnp.bfloat16)).astype(jnp.float32)
    attn_out = jnp.einsum("bkgqp,bpke->bqkge", probs_low, value_in)
    row_delta = jnp.transpose(jnp.sum(grad_in * attn_out, axis=-1), (0, 2, 3, 1))
    dprobs = jnp.einsum("bqkge,bpke->bkgqp", grad_in, value_in)
    dscores = (attn_probs * (dprobs - row_delta[..., None])).astype(jnp.bfloat16)
    dscores = lax.optimization_barrier(dscores).astype(jnp.float32)
    grad_query = (jnp.einsum("bkgqp,bpke->bqkge", dscores, key_in) * score_scale).astype(jnp.bfloat16)
    grad_key = (jnp.einsum("bkgqp,bqkge->bpke", dscores, query_in) * score_scale).astype(jnp.bfloat16)
    grad_value = jnp.einsum("bkgqp,bqkge->bpke", probs_low, grad_in).astype(jnp.bfloat16)
    return grad_query, grad_key, grad_value


def one_sequence(hidden, query_rows, grad_rows, key_w, value_w, lengths):
    key_rows = jnp.dot(hidden, key_w, preferred_element_type=jnp.float32).astype(jnp.bfloat16)
    value_rows = jnp.dot(hidden, value_w, preferred_element_type=jnp.float32).astype(jnp.bfloat16)
    doc_ends = jnp.cumsum(lengths)
    positions = jnp.arange(S, dtype=jnp.int32)
    segment = jnp.sum((positions[:, None] >= doc_ends[None, :]).astype(jnp.int32), axis=1)
    allowed = (segment[:, None] == segment[None, :]) & (positions[None, :] <= positions[:, None])
    query_shape = (1, S, KV, HEADS // KV, HD)
    key_shape = (1, S, KV, HD)
    grad_query, grad_key, grad_value = attend(
        query_rows.astype(jnp.float32).reshape(query_shape),
        grad_rows.astype(jnp.float32).reshape(query_shape),
        key_rows.astype(jnp.float32).reshape(key_shape),
        value_rows.astype(jnp.float32).reshape(key_shape),
        allowed[None])
    grad_query = grad_query.reshape(S, HEADS * HD)
    grad_key = grad_key.reshape(S, KV * HD)
    grad_value = grad_value.reshape(S, KV * HD)
    local_cols = KV * HD // N_TP
    layer_grad = jnp.zeros((S, D), jnp.float32)
    for member in range(N_TP):
        first_col = member * local_cols
        last_col = first_col + local_cols
        part_term = jnp.dot(grad_key[:, first_col:last_col], key_w[:, first_col:last_col].T, preferred_element_type=jnp.float32)
        part_term = part_term + jnp.dot(grad_value[:, first_col:last_col], value_w[:, first_col:last_col].T, preferred_element_type=jnp.float32)
        rounded = lax.optimization_barrier(part_term.astype(jnp.bfloat16))
        layer_grad = layer_grad + rounded.astype(jnp.float32)
    weight_scale = TOKENS ** -0.5
    key_term = (jnp.dot(hidden.T, grad_key, preferred_element_type=jnp.float32) * weight_scale).astype(jnp.bfloat16)
    value_term = (jnp.dot(hidden.T, grad_value, preferred_element_type=jnp.float32) * weight_scale).astype(jnp.bfloat16)
    key_term, value_term = lax.optimization_barrier((key_term, value_term))
    return grad_query, layer_grad.astype(jnp.bfloat16), key_term, value_term


def reference(hidden_in, queries, out_grad, key_weight, value_weight, doc_lengths):
    def per_section(section_in):
        hidden_s, query_s, grad_s, key_w, value_w, lengths_s = section_in

        def per_pipe(running, seq_in):
            grad_query, layer_grad, key_term, value_term = one_sequence(seq_in[0], seq_in[1], seq_in[2], key_w, value_w, seq_in[3])
            running = (running[0] + key_term.astype(jnp.float32), running[1] + value_term.astype(jnp.float32))
            return running, (grad_query, layer_grad)

        shaped = (hidden_s.reshape(PIPES, S, D), query_s.reshape(PIPES, S, HEADS * HD),
                  grad_s.reshape(PIPES, S, HEADS * HD), lengths_s)
        initial = (jnp.zeros((D, KV * HD), jnp.float32), jnp.zeros((D, KV * HD), jnp.float32))
        totals, rows_out = lax.scan(per_pipe, initial, shaped)
        return (rows_out[0].reshape(TOKENS, HEADS * HD), rows_out[1].reshape(TOKENS, D), totals[0], totals[1])

    query_grad, layer_grads, key_grad, value_grad = lax.map(
        per_section, (hidden_in, queries, out_grad, key_weight, value_weight, doc_lengths))
    return query_grad, jnp.roll(layer_grads, -1, axis=0), key_grad, value_grad
```

```python
import functools

import jax
import jax.numpy as jnp
from jax import lax
from jax.experimental import pallas as pl
from jax.experimental.pallas import tpu as pltpu
from jax.sharding import PartitionSpec as P

HD = 128
ROWS = 512
WIDTH = 8192
SHARD = 1024
HALF = 512
GROUP = 8
TILE = 512
TILES = 8
MESH = pl.DeviceIdType.MESH
NT = (((1,), (1,)), ((), ()))
TN = (((0,), (0,)), ((), ()))

GATHER = ("p0a", "p0b", "m0a", "m0b", "y0a", "y0b", "p1a", "m1b", "p2a", "p2b", "m2a", "m2b", "y2a", "y2b")
SCATTER = ("y1", "p1", "m1", "p2", "m2", "y3", "p3k", "p3v", "m3k", "m3v")
PER_HEAD = len(GATHER) + len(SCATTER)
TP_SEM = 2 * PER_HEAD
PP_SEM = TP_SEM + TILES
REMOTE_SEMS = PP_SEM + TILES
HID_SEM, Q_SEM, G_SEM, W_SEM, DQ_SEM, WG_SEM = 0, 8, 9, 10, 14, 16
LOCAL_SEMS = 18


def kernel(
    hidden_ref, query_ref, grad_ref, kw_ref, vw_ref, len_ref,
    dq_ref, lg_ref, wk_ref, wv_ref,
    hid, qs, gs, dqs, wg, kv, acc, bias, gacc, gkv, gkvt, prod,
    ry1, rp1, rm1, rp2, rm2, ry3, rp3, rm3,
    lgs, lgr, lgo, wks, wvs, ssem, rsem, lsem,
):
    dp, pp, tp = lax.axis_index("dp"), lax.axis_index("pp"), lax.axis_index("tp")
    x, y = dp // 2, dp % 2
    xp, xm, x2, yq = (x + 1) % 4, (x + 3) % 4, (x + 2) % 4, 1 - y
    j_me, j_p, j_m, j_2 = dp, xp * 2 + y, xm * 2 + y, x2 * 2 + y
    j_q, j_pq, j_mq, j_2q = x * 2 + yq, xp * 2 + yq, xm * 2 + yq, x2 * 2 + yq
    dev_p, dev_m, dev_y = (j_p, pp, tp), (j_m, pp, tp), (j_q, pp, tp)
    dev_t = (dp, pp, 1 - tp)
    dev_prev, dev_next = (dp, (pp + 7) % 8, tp), (dp, (pp + 1) % 8, tp)

    sent = []

    def remote(src, dst, k, dev):
        return pltpu.make_async_remote_copy(
            src_ref=src, dst_ref=dst, send_sem=ssem.at[k], recv_sem=rsem.at[k],
            device_id=dev, device_id_type=MESH,
        )

    def local(src, dst, k):
        return pltpu.make_async_copy(src, dst, lsem.at[k])

    w_copies = []
    for h in range(2):
        for n, ref in enumerate((kw_ref, vw_ref)):
            c = local(ref.at[:, pl.ds(h * HD, HD)], wg.at[h, j_me, :, pl.ds(n * HD, HD)], W_SEM + 2 * h + n)
            c.start()
            w_copies.append(c)
    hid_copies = []
    for j in range(8):
        c = local(hidden_ref.at[:, pl.ds(j * SHARD, SHARD)], hid.at[:, pl.ds(j * SHARD, SHARD)], HID_SEM + j)
        c.start()
        hid_copies.append(c)
    q_copy = local(query_ref, qs, Q_SEM)
    g_copy = local(grad_ref, gs, G_SEM)
    q_copy.start()
    g_copy.start()

    barrier = pltpu.get_barrier_semaphore()
    for dev in (dev_p, dev_m, dev_y, dev_t, dev_prev, dev_next):
        pl.semaphore_signal(barrier, inc=1, device_id=dev, device_id_type=MESH)
    pl.semaphore_wait(barrier, 6)

    def gather_copy(h, name):
        dev = {"p": dev_p, "m": dev_m, "y": dev_y}[name[0]]
        j = {"p0": j_me, "m0": j_me, "y0": j_me, "p1": j_m, "m1": j_p, "p2": j_q, "m2": j_q, "y2": j_2}[name[:2]]
        rows = pl.ds(0 if name[2] == "a" else HALF, HALF)
        block = wg.at[h, j, rows]
        return remote(block, block, h * PER_HEAD + GATHER.index(name), dev)

    def gather_start(h, *names):
        for name in names:
            c = gather_copy(h, name)
            c.start()
            sent.append(c)

    def gather_wait(h, *names):
        for name in names:
            gather_copy(h, name).wait_recv()

    def project(h, j, first=False):
        columns = pl.ds(pl.multiple_of(j * SHARD, SHARD), SHARD)
        term = jnp.dot(hid[:, columns], wg[h, j], preferred_element_type=jnp.float32)
        if first:
            acc[...] = term
        else:
            acc[...] += term

    def attend(h, b):
        w0 = 128 * max(b - 1, 0)
        window = pl.ds(w0, 256)

        def pair(i, carry):
            c0 = pl.multiple_of((h * GROUP + 2 * i) * HD, 2 * HD)
            rows = pl.ds(b * 128, 128)
            q2 = jnp.concatenate([qs[rows, pl.ds(c0, HD)], qs[rows, pl.ds(c0 + HD, HD)]], axis=0)
            g2 = jnp.concatenate([gs[rows, pl.ds(c0, HD)], gs[rows, pl.ds(c0 + HD, HD)]], axis=0)
            keys = kv[h, window, pl.ds(0, HD)]
            values = kv[h, window, pl.ds(HD, HD)]
            mask = bias[b]
            s = lax.dot_general(keys, q2, NT, preferred_element_type=jnp.float32)
            s = s * (HD ** -0.5) + jnp.concatenate([mask, mask], axis=1)
            top = jnp.max(s, axis=0, keepdims=True)
            e = jnp.exp(s - top)
            p = e * (1.0 / jnp.sum(e, axis=0, keepdims=True))
            low = p.astype(jnp.bfloat16)
            dpr = lax.dot_general(values, g2, NT, preferred_element_type=jnp.float32)
            delta = jnp.sum(low.astype(jnp.float32) * dpr, axis=0, keepdims=True)
            ds = (p * (dpr - delta)).astype(jnp.bfloat16)
            dq = lax.dot_general(ds, keys, TN, preferred_element_type=jnp.float32) * (HD ** -0.5)
            dq = dq.astype(jnp.bfloat16)
            dqs[rows, pl.ds(c0, HD)] = dq[:128]
            dqs[rows, pl.ds(c0 + HD, HD)] = dq[128:]
            gacc[window, pl.ds(0, HD)] += jnp.dot(ds, q2, preferred_element_type=jnp.float32)
            gacc[window, pl.ds(HD, HD)] += jnp.dot(low, g2, preferred_element_type=jnp.float32)
            return carry

        lax.fori_loop(0, GROUP // 2, pair, 0)

    def finish_head(h):
        columns = pl.ds(h * GROUP * HD, GROUP * HD)
        local(dqs.at[:, columns], dq_ref.at[:, columns], DQ_SEM + h).start()
        key_part = gacc[:, pl.ds(0, HD)] * (HD ** -0.5)
        value_part = gacc[:, pl.ds(HD, HD)]
        gkv[h, :, pl.ds(0, HD)] = key_part.astype(jnp.bfloat16)
        gkv[h, :, pl.ds(HD, HD)] = value_part.astype(jnp.bfloat16)
        gkvt[h, pl.ds(0, HD), :] = key_part.T.astype(jnp.bfloat16)
        gkvt[h, pl.ds(HD, HD), :] = value_part.T.astype(jnp.bfloat16)

    targets = (j_2q, j_pq, j_mq, j_2, j_q, j_p, j_m)

    def term(h, j):
        columns = pl.ds(pl.multiple_of(j * SHARD, SHARD), SHARD)
        out = jnp.dot(gkvt[h], hid[:, columns], preferred_element_type=jnp.float32)
        return (out * ((ROWS * 8) ** -0.5)).astype(jnp.bfloat16)

    def terms(h, *slots):
        for n in slots:
            prod[h, n] = term(h, targets[n])

    krows, vrows = pl.ds(0, HD), pl.ds(HD, HD)

    def scatter_copy(h, name):
        src, dst, dev = {
            "y1": (prod.at[h, 0], ry1.at[h], dev_y),
            "p1": (prod.at[h, 1], rp1.at[h], dev_p),
            "m1": (prod.at[h, 2], rm1.at[h], dev_m),
            "p2": (prod.at[h, 3, krows], rp2.at[h], dev_p),
            "m2": (prod.at[h, 3, vrows], rm2.at[h], dev_m),
            "y3": (prod.at[h, 4], ry3.at[h], dev_y),
            "p3k": (prod.at[h, 5, krows], rp3.at[h, krows], dev_p),
            "p3v": (prod.at[h, 5, vrows], rp3.at[h, vrows], dev_p),
            "m3k": (prod.at[h, 6, krows], rm3.at[h, krows], dev_m),
            "m3v": (prod.at[h, 6, vrows], rm3.at[h, vrows], dev_m),
        }[name]
        return remote(src, dst, h * PER_HEAD + len(GATHER) + SCATTER.index(name), dev)

    def scatter_start(h, *names):
        for name in names:
            c = scatter_copy(h, name)
            c.start()
            sent.append(c)

    def scatter_wait(h, *names):
        for name in names:
            scatter_copy(h, name).wait_recv()

    def wide(block):
        return block.astype(jnp.float32)

    def scatter_first(h):
        terms(h, 0, 1, 2)
        scatter_start(h, "y1", "p1", "m1")

    def scatter_rest_terms(h):
        terms(h, 3, 4, 5, 6)
        scatter_start(h, "p3v", "m3k")

    def scatter_second(h):
        scatter_wait(h, "y1")
        prod[h, 3] = (wide(prod[h, 3]) + wide(ry1[h])).astype(jnp.bfloat16)
        scatter_start(h, "p2", "m2")
        scatter_wait(h, "p1", "m1")
        prod[h, 4] = (wide(prod[h, 4]) + wide(rp1[h]) + wide(rm1[h])).astype(jnp.bfloat16)
        scatter_start(h, "y3")

    def scatter_third(h):
        scatter_wait(h, "p2", "m2")
        prod[h, 5, krows] = (wide(prod[h, 5, krows]) + wide(rp2[h])).astype(jnp.bfloat16)
        scatter_start(h, "p3k")
        prod[h, 6, vrows] = (wide(prod[h, 6, vrows]) + wide(rm2[h])).astype(jnp.bfloat16)
        scatter_start(h, "m3v")

    def scatter_last(h):
        own = term(h, j_me)
        scatter_wait(h, "y3", "p3k", "p3v", "m3k", "m3v")
        total = wide(own) + wide(ry3[h]) + wide(rp3[h]) + wide(rm3[h])
        wks[:, pl.ds(h * HD, HD)] = total[:HD].T
        wvs[:, pl.ds(h * HD, HD)] = total[HD:].T

    for c in w_copies:
        c.wait()
    gather_start(0, "p0a", "p0b", "m0a", "m0b", "y0a", "y0b")
    ends, last = [], jnp.int32(0)
    for k in range(8):
        last = last + len_ref[0, k]
        ends.append(last)
    for b in range(4):
        w0 = 128 * max(b - 1, 0)
        key_at = lax.broadcasted_iota(jnp.int32, (256, 128), 0) + w0
        query_at = lax.broadcasted_iota(jnp.int32, (256, 128), 1) + b * 128
        key_doc = jnp.zeros((256, 128), jnp.int32)
        query_doc = jnp.zeros((256, 128), jnp.int32)
        for end in ends:
            key_doc += (key_at >= end).astype(jnp.int32)
            query_doc += (query_at >= end).astype(jnp.int32)
        bias[b] = jnp.where((key_doc == query_doc) & (key_at <= query_at), 0.0, -1e30)
    for c in hid_copies:
        c.wait()
    project(0, j_me, True)
    gather_wait(0, "p0a", "m0a")
    gather_start(0, "p1a")
    gather_wait(0, "y0a")
    gather_start(0, "p2a", "m2a")
    gather_wait(0, "m0b")
    gather_start(0, "m1b")
    gather_wait(0, "p0b", "y0b")
    gather_start(0, "p2b", "m2b")
    for j in (j_m, j_p, j_q):
        project(0, j)
    gather_wait(0, "p1a")
    gather_start(0, "y2a")
    gather_wait(0, "m1b")
    gather_start(0, "y2b")
    project(0, j_2)
    gather_wait(0, "p2a", "m2a")
    gather_start(1, "p0a", "p0b", "m0a", "m0b")
    gather_wait(0, "y2a")
    gather_start(1, "y0a", "y0b")
    gather_wait(0, "p2b", "m2b")
    project(0, j_pq)
    project(0, j_mq)
    gather_wait(0, "y2b")
    project(0, j_2q)
    kv[0] = acc[...].astype(jnp.bfloat16)
    q_copy.wait()
    g_copy.wait()

    gacc[...] = jnp.zeros_like(gacc)
    attend(0, 0)
    gather_wait(1, "p0a", "m0a")
    gather_start(1, "p1a")
    gather_wait(1, "y0a")
    gather_start(1, "p2a", "m2a")
    attend(0, 1)
    gather_wait(1, "m0b")
    gather_start(1, "m1b")
    gather_wait(1, "p0b", "y0b")
    gather_start(1, "p2b", "m2b")
    attend(0, 2)
    gather_wait(1, "p1a")
    gather_start(1, "y2a")
    gather_wait(1, "m1b")
    gather_start(1, "y2b")
    attend(0, 3)
    finish_head(0)
    terms(0, 0, 1, 2)
    project(1, j_me, True)
    for j in (j_m, j_p, j_q, j_2):
        project(1, j)
    gather_wait(1, "p2a", "m2a", "y2a")
    scatter_start(0, "y1", "p1", "m1")
    terms(0, 3, 4, 5, 6)
    gather_wait(1, "p2b", "m2b")
    project(1, j_pq)
    project(1, j_mq)
    gather_wait(1, "y2b")
    project(1, j_2q)
    kv[1] = acc[...].astype(jnp.bfloat16)
    scatter_start(0, "p3v", "m3k")

    gacc[...] = jnp.zeros_like(gacc)
    attend(1, 0)
    attend(1, 1)
    scatter_second(0)
    attend(1, 2)
    attend(1, 3)
    finish_head(1)

    def tp_copy(t):
        return remote(lgs.at[t], lgr.at[t], TP_SEM + t, dev_t)

    def pp_copy(t):
        columns = pl.ds(pl.multiple_of(t * TILE, TILE), TILE)
        return remote(lgo.at[t], lg_ref.at[:, columns], PP_SEM + t, dev_prev)

    def layer_tile(half, t):
        j = half * 4 + t // 2
        rows = pl.ds(pl.multiple_of((t % 2) * TILE, TILE), TILE)
        return lax.dot_general(gkv[0], wg[0, j, rows], NT, preferred_element_type=jnp.float32) + lax.dot_general(
            gkv[1], wg[1, j, rows], NT, preferred_element_type=jnp.float32
        )

    def layer_step(t, carry):
        @pl.when(t < TILES)
        def _():
            lgs[t] = layer_tile(1 - tp, t).astype(jnp.bfloat16)
            tp_copy(t).start()
            lgo[t] = layer_tile(tp, t).astype(jnp.bfloat16)

        @pl.when(t > 0)
        def _():
            tp_copy(t - 1).wait_recv()
            lgo[t - 1] = (wide(lgo[t - 1]) + wide(lgr[t - 1])).astype(jnp.bfloat16)
            pp_copy(t - 1).start()

        return carry

    lax.fori_loop(0, TILES + 1, layer_step, 0)

    scatter_third(0)
    terms(1, 0, 1, 2)
    scatter_start(1, "y1", "p1", "m1")
    scatter_last(0)
    scatter_rest_terms(1)
    scatter_second(1)
    scatter_third(1)
    scatter_last(1)
    wk_copy = local(wks, wk_ref, WG_SEM)
    wv_copy = local(wvs, wv_ref, WG_SEM + 1)
    wk_copy.start()
    wv_copy.start()
    for c in sent:
        c.wait_send()

    def drain(t, carry):
        tp_copy(t).wait_send()
        pp_copy(t).wait_send()
        pp_copy(t).wait_recv()
        return carry

    lax.fori_loop(0, TILES, drain, 0)
    for h in range(2):
        columns = pl.ds(h * GROUP * HD, GROUP * HD)
        local(dqs.at[:, columns], dq_ref.at[:, columns], DQ_SEM + h).wait()
    wk_copy.wait()
    wv_copy.wait()


def body(hidden_in, queries, out_grad, key_weight, value_weight, doc_lengths):
    any_space = pl.BlockSpec(memory_space=pl.ANY)
    bf16, f32 = jnp.bfloat16, jnp.float32
    block = (2, 2 * HD, SHARD)
    outs = pl.pallas_call(
        kernel,
        out_shape=(
            jax.ShapeDtypeStruct((ROWS, 2048), bf16),
            jax.ShapeDtypeStruct((ROWS, WIDTH // 2), bf16),
            jax.ShapeDtypeStruct((SHARD, 2 * HD), f32),
            jax.ShapeDtypeStruct((SHARD, 2 * HD), f32),
        ),
        in_specs=[any_space] * 5 + [pl.BlockSpec(memory_space=pltpu.SMEM)],
        out_specs=(any_space,) * 4,
        scratch_shapes=[
            pltpu.VMEM((ROWS, WIDTH), bf16),
            pltpu.VMEM((ROWS, 2048), bf16),
            pltpu.VMEM((ROWS, 2048), bf16),
            pltpu.VMEM((ROWS, 2048), bf16),
            pltpu.VMEM((2, 8, SHARD, 2 * HD), bf16),
            pltpu.VMEM((2, ROWS, 2 * HD), bf16),
            pltpu.VMEM((ROWS, 2 * HD), f32),
            pltpu.VMEM((4, 256, 128), f32),
            pltpu.VMEM((ROWS, 2 * HD), f32),
            pltpu.VMEM((2, ROWS, 2 * HD), bf16),
            pltpu.VMEM((2, 2 * HD, ROWS), bf16),
            pltpu.VMEM((2, 7, 2 * HD, SHARD), bf16),
            pltpu.VMEM(block, bf16),
            pltpu.VMEM(block, bf16),
            pltpu.VMEM(block, bf16),
            pltpu.VMEM((2, HD, SHARD), bf16),
            pltpu.VMEM((2, HD, SHARD), bf16),
            pltpu.VMEM(block, bf16),
            pltpu.VMEM(block, bf16),
            pltpu.VMEM(block, bf16),
            pltpu.VMEM((TILES, ROWS, TILE), bf16),
            pltpu.VMEM((TILES, ROWS, TILE), bf16),
            pltpu.VMEM((TILES, ROWS, TILE), bf16),
            pltpu.VMEM((SHARD, 2 * HD), f32),
            pltpu.VMEM((SHARD, 2 * HD), f32),
            pltpu.SemaphoreType.DMA((REMOTE_SEMS,)),
            pltpu.SemaphoreType.DMA((REMOTE_SEMS,)),
            pltpu.SemaphoreType.DMA((LOCAL_SEMS,)),
        ],
        compiler_params=pltpu.CompilerParams(
            collective_id=0, has_side_effects=True, vmem_limit_bytes=62 * 1024 * 1024
        ),
        cost_estimate=pl.CostEstimate(flops=18_000_000_000, bytes_accessed=24_000_000, transcendentals=2_100_000),
    )(hidden_in[0], queries[0], out_grad[0], key_weight[0], value_weight[0], doc_lengths[0])
    return tuple(out[None] for out in outs)


def solution(mesh):
    return jax.shard_map(
        body,
        mesh=mesh,
        in_specs=(
            P("pp", "dp", None),
            P("pp", "dp", "tp"),
            P("pp", "dp", "tp"),
            P("pp", "dp", "tp"),
            P("pp", "dp", "tp"),
            P("pp", "dp", None),
        ),
        out_specs=(
            P("pp", "dp", "tp"),
            P("pp", "dp", "tp"),
            P("pp", "dp", "tp"),
            P("pp", "dp", "tp"),
        ),
        check_vma=False,
    )
```

```python
import functools

import jax
import jax.numpy as jnp
from jax import lax
from jax.experimental import pallas as pl
from jax.experimental.pallas import tpu as pltpu
from jax.sharding import PartitionSpec as P

HD = 128
ROWS = 512
WIDTH = 8192
SHARD = 1024
HALF = 512
GROUP = 8
TILE = 512
TILES = 8
MESH = pl.DeviceIdType.MESH
NT = (((1,), (1,)), ((), ()))
TN = (((0,), (0,)), ((), ()))

GATHER = ("p0a", "p0b", "m0a", "m0b", "y0a", "y0b", "p1a", "m1b", "p2a", "p2b", "m2a", "m2b", "y2a", "y2b")
SCATTER = ("y1", "p1", "m1", "p2", "m2", "y3", "p3k", "p3v", "m3k", "m3v")
PER_HEAD = len(GATHER) + len(SCATTER)
TP_SEM = 2 * PER_HEAD
PP_SEM = TP_SEM + TILES
HOP1_SEM = PP_SEM + TILES
HOP2_SEM = HOP1_SEM + 2
HOP3_SEM = HOP2_SEM + 2
RELAY_SEM = HOP3_SEM + 2
PASS_SEM = RELAY_SEM + 3
REMOTE_SEMS = PASS_SEM + 3
LONG_TILES = (1, 3)
RELAY_TILES = (0, 4, 6)
HID_SEM, Q_SEM, G_SEM, W_SEM, DQ_SEM, WG_SEM = 0, 8, 9, 10, 14, 16
LOCAL_SEMS = 18


def kernel(
    hidden_ref, query_ref, grad_ref, kw_ref, vw_ref, len_ref,
    dq_ref, lg_ref, wk_ref, wv_ref,
    hid, qs, gs, dqs, wg, kv, acc, bias, gacc, gkv, gkvt, prod,
    ry1, rp1, rm1, rp2, rm2, ry3, rp3, rm3,
    lgs, lgr, lgo, hop1, hop2, held, wks, wvs, ssem, rsem, lsem,
):
    dp, pp, tp = lax.axis_index("dp"), lax.axis_index("pp"), lax.axis_index("tp")
    x, y = dp // 2, dp % 2
    xp, xm, x2, yq = (x + 1) % 4, (x + 3) % 4, (x + 2) % 4, 1 - y
    j_me, j_p, j_m, j_2 = dp, xp * 2 + y, xm * 2 + y, x2 * 2 + y
    j_q, j_pq, j_mq, j_2q = x * 2 + yq, xp * 2 + yq, xm * 2 + yq, x2 * 2 + yq
    dev_p, dev_m, dev_y = (j_p, pp, tp), (j_m, pp, tp), (j_q, pp, tp)
    dev_t = (dp, pp, 1 - tp)
    hi, z = pp // 4, pp % 4
    z_up, z_down = (z + 1) % 4, (z + 3) % 4
    dev_prev = (dp, (pp + 7) % 8, tp)
    dev_up, dev_down = (dp, hi * 4 + z_up, tp), (dp, hi * 4 + z_down, tp)
    dev_far = (dp, (1 - hi) * 4 + z, tp)
    dev_far_up, dev_far_down = (dp, (1 - hi) * 4 + z_up, tp), (dp, (1 - hi) * 4 + z_down, tp)
    dev_hop3 = (dp, jnp.where(z == 2, 1 - hi, hi) * 4 + z_up, tp)

    sent = []

    def remote(src, dst, k, dev, arrival=None):
        return pltpu.make_async_remote_copy(
            src_ref=src, dst_ref=dst, send_sem=ssem.at[k], recv_sem=rsem.at[k if arrival is None else arrival],
            device_id=dev, device_id_type=MESH,
        )

    def local(src, dst, k):
        return pltpu.make_async_copy(src, dst, lsem.at[k])

    w_copies = []
    for h in range(2):
        for n, ref in enumerate((kw_ref, vw_ref)):
            c = local(ref.at[:, pl.ds(h * HD, HD)], wg.at[h, j_me, :, pl.ds(n * HD, HD)], W_SEM + 2 * h + n)
            c.start()
            w_copies.append(c)
    hid_copies = []
    for j in range(8):
        c = local(hidden_ref.at[:, pl.ds(j * SHARD, SHARD)], hid.at[:, pl.ds(j * SHARD, SHARD)], HID_SEM + j)
        c.start()
        hid_copies.append(c)
    q_copy = local(query_ref, qs, Q_SEM)
    g_copy = local(grad_ref, gs, G_SEM)
    q_copy.start()
    g_copy.start()

    barrier = pltpu.get_barrier_semaphore()
    for dev in (dev_p, dev_m, dev_y, dev_t, dev_up, dev_down, dev_far, dev_far_up, dev_far_down):
        pl.semaphore_signal(barrier, inc=1, device_id=dev, device_id_type=MESH)
    pl.semaphore_wait(barrier, 9)

    def gather_copy(h, name):
        dev = {"p": dev_p, "m": dev_m, "y": dev_y}[name[0]]
        j = {"p0": j_me, "m0": j_me, "y0": j_me, "p1": j_m, "m1": j_p, "p2": j_q, "m2": j_q, "y2": j_2}[name[:2]]
        rows = pl.ds(0 if name[2] == "a" else HALF, HALF)
        block = wg.at[h, j, rows]
        return remote(block, block, h * PER_HEAD + GATHER.index(name), dev)

    def gather_start(h, *names):
        for name in names:
            c = gather_copy(h, name)
            c.start()
            sent.append(c)

    def gather_wait(h, *names):
        for name in names:
            gather_copy(h, name).wait_recv()

    def project(h, j, first=False):
        columns = pl.ds(pl.multiple_of(j * SHARD, SHARD), SHARD)
        term = jnp.dot(hid[:, columns], wg[h, j], preferred_element_type=jnp.float32)
        if first:
            acc[...] = term
        else:
            acc[...] += term

    def attend(h, b):
        w0 = 128 * max(b - 1, 0)
        window = pl.ds(w0, 256)

        def pair(i, carry):
            c0 = pl.multiple_of((h * GROUP + 2 * i) * HD, 2 * HD)
            rows = pl.ds(b * 128, 128)
            q2 = jnp.concatenate([qs[rows, pl.ds(c0, HD)], qs[rows, pl.ds(c0 + HD, HD)]], axis=0)
            g2 = jnp.concatenate([gs[rows, pl.ds(c0, HD)], gs[rows, pl.ds(c0 + HD, HD)]], axis=0)
            keys = kv[h, window, pl.ds(0, HD)]
            values = kv[h, window, pl.ds(HD, HD)]
            mask = bias[b]
            s = lax.dot_general(keys, q2, NT, preferred_element_type=jnp.float32)
            s = s * (HD ** -0.5) + jnp.concatenate([mask, mask], axis=1)
            top = jnp.max(s, axis=0, keepdims=True)
            e = jnp.exp(s - top)
            p = e * (1.0 / jnp.sum(e, axis=0, keepdims=True))
            low = p.astype(jnp.bfloat16)
            dpr = lax.dot_general(values, g2, NT, preferred_element_type=jnp.float32)
            delta = jnp.sum(low.astype(jnp.float32) * dpr, axis=0, keepdims=True)
            ds = (p * (dpr - delta)).astype(jnp.bfloat16)
            dq = lax.dot_general(ds, keys, TN, preferred_element_type=jnp.float32) * (HD ** -0.5)
            dq = dq.astype(jnp.bfloat16)
            dqs[rows, pl.ds(c0, HD)] = dq[:128]
            dqs[rows, pl.ds(c0 + HD, HD)] = dq[128:]
            gacc[window, pl.ds(0, HD)] += jnp.dot(ds, q2, preferred_element_type=jnp.float32)
            gacc[window, pl.ds(HD, HD)] += jnp.dot(low, g2, preferred_element_type=jnp.float32)
            return carry

        lax.fori_loop(0, GROUP // 2, pair, 0)

    def finish_head(h):
        columns = pl.ds(h * GROUP * HD, GROUP * HD)
        local(dqs.at[:, columns], dq_ref.at[:, columns], DQ_SEM + h).start()
        key_part = gacc[:, pl.ds(0, HD)] * (HD ** -0.5)
        value_part = gacc[:, pl.ds(HD, HD)]
        gkv[h, :, pl.ds(0, HD)] = key_part.astype(jnp.bfloat16)
        gkv[h, :, pl.ds(HD, HD)] = value_part.astype(jnp.bfloat16)
        gkvt[h, pl.ds(0, HD), :] = key_part.T.astype(jnp.bfloat16)
        gkvt[h, pl.ds(HD, HD), :] = value_part.T.astype(jnp.bfloat16)

    targets = (j_2q, j_pq, j_mq, j_2, j_q, j_p, j_m)

    def term(h, j):
        columns = pl.ds(pl.multiple_of(j * SHARD, SHARD), SHARD)
        out = jnp.dot(gkvt[h], hid[:, columns], preferred_element_type=jnp.float32)
        return (out * ((ROWS * 8) ** -0.5)).astype(jnp.bfloat16)

    def terms(h, *slots):
        for n in slots:
            prod[h, n] = term(h, targets[n])

    krows, vrows = pl.ds(0, HD), pl.ds(HD, HD)

    def scatter_copy(h, name):
        src, dst, dev = {
            "y1": (prod.at[h, 0], ry1.at[h], dev_y),
            "p1": (prod.at[h, 1], rp1.at[h], dev_p),
            "m1": (prod.at[h, 2], rm1.at[h], dev_m),
            "p2": (prod.at[h, 3, krows], rp2.at[h], dev_p),
            "m2": (prod.at[h, 3, vrows], rm2.at[h], dev_m),
            "y3": (prod.at[h, 4], ry3.at[h], dev_y),
            "p3k": (prod.at[h, 5, krows], rp3.at[h, krows], dev_p),
            "p3v": (prod.at[h, 5, vrows], rp3.at[h, vrows], dev_p),
            "m3k": (prod.at[h, 6, krows], rm3.at[h, krows], dev_m),
            "m3v": (prod.at[h, 6, vrows], rm3.at[h, vrows], dev_m),
        }[name]
        return remote(src, dst, h * PER_HEAD + len(GATHER) + SCATTER.index(name), dev)

    def scatter_start(h, *names):
        for name in names:
            c = scatter_copy(h, name)
            c.start()
            sent.append(c)

    def scatter_wait(h, *names):
        for name in names:
            scatter_copy(h, name).wait_recv()

    def wide(block):
        return block.astype(jnp.float32)

    def scatter_first(h):
        terms(h, 0, 1, 2)
        scatter_start(h, "y1", "p1", "m1")

    def scatter_rest_terms(h):
        terms(h, 3, 4, 5, 6)
        scatter_start(h, "p3v", "m3k")

    def scatter_second(h):
        scatter_wait(h, "y1")
        prod[h, 3] = (wide(prod[h, 3]) + wide(ry1[h])).astype(jnp.bfloat16)
        scatter_start(h, "p2", "m2")
        scatter_wait(h, "p1", "m1")
        prod[h, 4] = (wide(prod[h, 4]) + wide(rp1[h]) + wide(rm1[h])).astype(jnp.bfloat16)
        scatter_start(h, "y3")

    def scatter_third(h):
        scatter_wait(h, "p2", "m2")
        prod[h, 5, krows] = (wide(prod[h, 5, krows]) + wide(rp2[h])).astype(jnp.bfloat16)
        scatter_start(h, "p3k")
        prod[h, 6, vrows] = (wide(prod[h, 6, vrows]) + wide(rm2[h])).astype(jnp.bfloat16)
        scatter_start(h, "m3v")

    def scatter_last(h):
        own = term(h, j_me)
        scatter_wait(h, "y3", "p3k", "p3v", "m3k", "m3v")
        total = wide(own) + wide(ry3[h]) + wide(rp3[h]) + wide(rm3[h])
        wks[:, pl.ds(h * HD, HD)] = total[:HD].T
        wvs[:, pl.ds(h * HD, HD)] = total[HD:].T

    for c in w_copies[:2]:
        c.wait()
    gather_start(0, "p0a", "m0b", "y0a", "p0b", "m0a", "y0b")
    for c in w_copies[2:]:
        c.wait()
    ends, last = [], jnp.int32(0)
    for k in range(8):
        last = last + len_ref[0, k]
        ends.append(last)
    for b in range(4):
        w0 = 128 * max(b - 1, 0)
        key_at = lax.broadcasted_iota(jnp.int32, (256, 128), 0) + w0
        query_at = lax.broadcasted_iota(jnp.int32, (256, 128), 1) + b * 128
        key_doc = jnp.zeros((256, 128), jnp.int32)
        query_doc = jnp.zeros((256, 128), jnp.int32)
        for end in ends:
            key_doc += (key_at >= end).astype(jnp.int32)
            query_doc += (query_at >= end).astype(jnp.int32)
        bias[b] = jnp.where((key_doc == query_doc) & (key_at <= query_at), 0.0, -1e30)
    for c in hid_copies:
        c.wait()
    project(0, j_me, True)
    gather_wait(0, "p0a", "m0b")
    gather_start(0, "p1a", "m1b")
    gather_wait(0, "y0a")
    gather_start(0, "p2a", "m2a")
    gather_wait(0, "m0a")
    gather_wait(0, "p0b", "y0b")
    gather_start(0, "p2b", "m2b")
    for j in (j_m, j_p, j_q):
        project(0, j)
    gather_wait(0, "p1a")
    gather_start(0, "y2a")
    gather_wait(0, "m1b")
    gather_start(0, "y2b")
    project(0, j_2)
    gather_wait(0, "p2a", "m2a")
    gather_start(1, "p0a", "m0b", "p0b", "m0a")
    gather_wait(0, "y2a")
    gather_start(1, "y0a", "y0b")
    gather_wait(0, "p2b", "m2b")
    project(0, j_pq)
    project(0, j_mq)
    gather_wait(0, "y2b")
    project(0, j_2q)
    kv[0] = acc[...].astype(jnp.bfloat16)
    q_copy.wait()
    g_copy.wait()

    gacc[...] = jnp.zeros_like(gacc)
    attend(0, 0)
    gather_wait(1, "p0a", "m0b")
    gather_start(1, "p1a", "m1b")
    gather_wait(1, "y0a")
    gather_start(1, "p2a", "m2a")
    attend(0, 1)
    gather_wait(1, "m0a")
    gather_wait(1, "p0b", "y0b")
    gather_start(1, "p2b", "m2b")
    attend(0, 2)
    gather_wait(1, "p1a")
    gather_start(1, "y2a")
    gather_wait(1, "m1b")
    gather_start(1, "y2b")
    attend(0, 3)
    finish_head(0)
    terms(0, 0, 1, 2)
    project(1, j_me, True)
    for j in (j_m, j_p, j_q, j_2):
        project(1, j)
    gather_wait(1, "p2a", "m2a", "y2a")
    scatter_start(0, "y1", "p1", "m1")
    terms(0, 3, 4, 5, 6)
    gather_wait(1, "p2b", "m2b")
    project(1, j_pq)
    project(1, j_mq)
    gather_wait(1, "y2b")
    project(1, j_2q)
    kv[1] = acc[...].astype(jnp.bfloat16)
    scatter_start(0, "p3v", "m3k")

    gacc[...] = jnp.zeros_like(gacc)
    attend(1, 0)
    attend(1, 1)
    attend(1, 2)
    attend(1, 3)
    finish_head(1)

    def tp_copy(t):
        return remote(lgs.at[t], lgr.at[t], TP_SEM + t, dev_t)

    def out_tile(t):
        return lg_ref.at[:, pl.ds(pl.multiple_of(t * TILE, TILE), TILE)]

    def pp_copy(t):
        return remote(lgo.at[t], out_tile(t), PP_SEM + t, dev_prev)

    def relay_copy(i, t):
        return remote(lgo.at[t], held.at[i], RELAY_SEM + i, dev_down)

    def pass_copy(i, t):
        return remote(held.at[i], out_tile(t), PASS_SEM + i, dev_far, PP_SEM + t)

    def hop1_copy(i, t):
        return remote(lgo.at[t], hop1.at[i], HOP1_SEM + i, dev_up)

    def hop2_copy(i):
        return remote(hop1.at[i], hop2.at[i], HOP2_SEM + i, dev_up)

    def hop3_copy(i, t):
        return remote(hop2.at[i], out_tile(t), HOP3_SEM + i, dev_hop3, PP_SEM + t)

    def second_hop(i):
        hop1_copy(i, LONG_TILES[i]).wait_recv()
        hop2_copy(i).start()

    def third_hop(i):
        hop2_copy(i).wait_recv()
        hop3_copy(i, LONG_TILES[i]).start()

    def pass_on(i):
        @pl.when(z == 3)
        def _():
            relay_copy(i, RELAY_TILES[i]).wait_recv()
            pass_copy(i, RELAY_TILES[i]).start()

    def send_tile(t):
        is_long = (t == LONG_TILES[0]) | (t == LONG_TILES[1])
        is_relay = (z == 0) & ((t == RELAY_TILES[0]) | (t == RELAY_TILES[1]) | (t == RELAY_TILES[2]))

        @pl.when(is_long)
        def _():
            hop1_copy(t // 2, t).start()

        @pl.when(is_relay)
        def _():
            relay_copy(jnp.maximum(t // 2 - 1, 0), t).start()

        @pl.when(jnp.logical_not(is_long | is_relay))
        def _():
            pp_copy(t).start()

    def layer_tile(half, t):
        j = half * 4 + t // 2
        rows = pl.ds(pl.multiple_of((t % 2) * TILE, TILE), TILE)
        return lax.dot_general(gkv[0], wg[0, j, rows], NT, preferred_element_type=jnp.float32) + lax.dot_general(
            gkv[1], wg[1, j, rows], NT, preferred_element_type=jnp.float32
        )

    def layer_step(t, carry):
        @pl.when(t < TILES)
        def _():
            lgs[t] = layer_tile(1 - tp, t).astype(jnp.bfloat16)
            tp_copy(t).start()
            lgo[t] = layer_tile(tp, t).astype(jnp.bfloat16)

        @pl.when(t > 0)
        def _():
            tp_copy(t - 1).wait_recv()
            lgo[t - 1] = (wide(lgo[t - 1]) + wide(lgr[t - 1])).astype(jnp.bfloat16)
            send_tile(t - 1)

        return carry

    lax.fori_loop(0, TILES + 1, layer_step, 0)

    scatter_second(0)
    terms(1, 0, 1, 2)
    scatter_start(1, "y1", "p1", "m1")
    scatter_third(0)
    scatter_rest_terms(1)
    second_hop(0)
    pass_on(0)
    scatter_last(0)
    scatter_second(1)
    second_hop(1)
    scatter_third(1)
    third_hop(0)
    pass_on(1)
    scatter_last(1)
    wk_copy = local(wks, wk_ref, WG_SEM)
    wv_copy = local(wvs, wv_ref, WG_SEM + 1)
    wk_copy.start()
    wv_copy.start()
    third_hop(1)
    pass_on(2)
    for c in sent:
        c.wait_send()
    for t in range(TILES):
        tp_copy(t).wait_send()
    for i, t in enumerate(LONG_TILES):
        hop1_copy(i, t).wait_send()
        hop2_copy(i).wait_send()
        hop3_copy(i, t).wait_send()
    for t in range(TILES):
        if t in LONG_TILES:
            continue
        if t not in RELAY_TILES:
            pp_copy(t).wait_send()
            continue
        i = RELAY_TILES.index(t)

        @pl.when(z == 0)
        def _(i=i, t=t):
            relay_copy(i, t).wait_send()

        @pl.when(z != 0)
        def _(t=t):
            pp_copy(t).wait_send()

        @pl.when(z == 3)
        def _(i=i, t=t):
            pass_copy(i, t).wait_send()

    for t in range(TILES):
        pp_copy(t).wait_recv()
    for h in range(2):
        columns = pl.ds(h * GROUP * HD, GROUP * HD)
        local(dqs.at[:, columns], dq_ref.at[:, columns], DQ_SEM + h).wait()
    wk_copy.wait()
    wv_copy.wait()


def body(hidden_in, queries, out_grad, key_weight, value_weight, doc_lengths):
    any_space = pl.BlockSpec(memory_space=pl.ANY)
    bf16, f32 = jnp.bfloat16, jnp.float32
    block = (2, 2 * HD, SHARD)
    outs = pl.pallas_call(
        kernel,
        out_shape=(
            jax.ShapeDtypeStruct((ROWS, 2048), bf16),
            jax.ShapeDtypeStruct((ROWS, WIDTH // 2), bf16),
            jax.ShapeDtypeStruct((SHARD, 2 * HD), f32),
            jax.ShapeDtypeStruct((SHARD, 2 * HD), f32),
        ),
        in_specs=[any_space] * 5 + [pl.BlockSpec(memory_space=pltpu.SMEM)],
        out_specs=(any_space,) * 4,
        scratch_shapes=[
            pltpu.VMEM((ROWS, WIDTH), bf16),
            pltpu.VMEM((ROWS, 2048), bf16),
            pltpu.VMEM((ROWS, 2048), bf16),
            pltpu.VMEM((ROWS, 2048), bf16),
            pltpu.VMEM((2, 8, SHARD, 2 * HD), bf16),
            pltpu.VMEM((2, ROWS, 2 * HD), bf16),
            pltpu.VMEM((ROWS, 2 * HD), f32),
            pltpu.VMEM((4, 256, 128), f32),
            pltpu.VMEM((ROWS, 2 * HD), f32),
            pltpu.VMEM((2, ROWS, 2 * HD), bf16),
            pltpu.VMEM((2, 2 * HD, ROWS), bf16),
            pltpu.VMEM((2, 7, 2 * HD, SHARD), bf16),
            pltpu.VMEM(block, bf16),
            pltpu.VMEM(block, bf16),
            pltpu.VMEM(block, bf16),
            pltpu.VMEM((2, HD, SHARD), bf16),
            pltpu.VMEM((2, HD, SHARD), bf16),
            pltpu.VMEM(block, bf16),
            pltpu.VMEM(block, bf16),
            pltpu.VMEM(block, bf16),
            pltpu.VMEM((TILES, ROWS, TILE), bf16),
            pltpu.VMEM((TILES, ROWS, TILE), bf16),
            pltpu.VMEM((TILES, ROWS, TILE), bf16),
            pltpu.VMEM((2, ROWS, TILE), bf16),
            pltpu.VMEM((2, ROWS, TILE), bf16),
            pltpu.VMEM((3, ROWS, TILE), bf16),
            pltpu.VMEM((SHARD, 2 * HD), f32),
            pltpu.VMEM((SHARD, 2 * HD), f32),
            pltpu.SemaphoreType.DMA((REMOTE_SEMS,)),
            pltpu.SemaphoreType.DMA((REMOTE_SEMS,)),
            pltpu.SemaphoreType.DMA((LOCAL_SEMS,)),
        ],
        compiler_params=pltpu.CompilerParams(
            collective_id=0, has_side_effects=True, vmem_limit_bytes=62 * 1024 * 1024
        ),
        cost_estimate=pl.CostEstimate(flops=18_000_000_000, bytes_accessed=24_000_000, transcendentals=2_100_000),
    )(hidden_in[0], queries[0], out_grad[0], key_weight[0], value_weight[0], doc_lengths[0])
    return tuple(out[None] for out in outs)


def solution(mesh):
    return jax.shard_map(
        body,
        mesh=mesh,
        in_specs=(
            P("pp", "dp", None),
            P("pp", "dp", "tp"),
            P("pp", "dp", "tp"),
            P("pp", "dp", "tp"),
            P("pp", "dp", "tp"),
            P("pp", "dp", None),
        ),
        out_specs=(
            P("pp", "dp", "tp"),
            P("pp", "dp", "tp"),
            P("pp", "dp", "tp"),
            P("pp", "dp", "tp"),
        ),
        check_vma=False,
    )
```

```python
import functools

import jax
import jax.numpy as jnp
from jax import lax
from jax.experimental import pallas as pl
from jax.experimental.pallas import tpu as pltpu
from jax.sharding import PartitionSpec as P

HD = 128
ROWS = 512
WIDTH = 8192
SHARD = 1024
HALF = 512
GROUP = 8
TILE = 512
TILES = 8
MESH = pl.DeviceIdType.MESH
NT = (((1,), (1,)), ((), ()))
TN = (((0,), (0,)), ((), ()))

GATHER = ("p0a", "p0b", "m0a", "m0b", "y0a", "y0b", "p1a", "m1b", "p2a", "p2b", "m2a", "m2b", "y2a", "y2b")
SCATTER = ("y1", "p1", "m1", "p2", "m2", "y3", "p3k", "p3v", "m3k", "m3v")
PER_HEAD = len(GATHER) + len(SCATTER)
TP_SEM = 2 * PER_HEAD
PP_SEM = TP_SEM + TILES
HOP1_SEM = PP_SEM + TILES
HOP2_SEM = HOP1_SEM + 2
HOP3_SEM = HOP2_SEM + 2
RELAY_SEM = HOP3_SEM + 2
PASS_SEM = RELAY_SEM + 3
REMOTE_SEMS = PASS_SEM + 3
LONG_TILES = (1, 3)
RELAY_TILES = (0, 2, 4)
DIRECT_TILES = (5, 6, 7)
HID_SEM, Q_SEM, G_SEM, W_SEM, DQ_SEM, WG_SEM = 0, 8, 9, 10, 14, 16
LOCAL_SEMS = 18


def kernel(
    hidden_ref, query_ref, grad_ref, kw_ref, vw_ref, len_ref,
    dq_ref, lg_ref, wk_ref, wv_ref,
    hid, qs, gs, dqs, wg, kv, acc, bias, gacc, gkv, gkvt, prod,
    ry1, rp1, rm1, rp2, rm2, ry3, rp3, rm3,
    lgs, lgr, lgo, hop1, hop2, held, wks, wvs, ssem, rsem, lsem,
):
    dp, pp, tp = lax.axis_index("dp"), lax.axis_index("pp"), lax.axis_index("tp")
    x, y = dp // 2, dp % 2
    xp, xm, x2, yq = (x + 1) % 4, (x + 3) % 4, (x + 2) % 4, 1 - y
    j_me, j_p, j_m, j_2 = dp, xp * 2 + y, xm * 2 + y, x2 * 2 + y
    j_q, j_pq, j_mq, j_2q = x * 2 + yq, xp * 2 + yq, xm * 2 + yq, x2 * 2 + yq
    dev_p, dev_m, dev_y = (j_p, pp, tp), (j_m, pp, tp), (j_q, pp, tp)
    dev_t = (dp, pp, 1 - tp)
    hi, z = pp // 4, pp % 4
    z_up, z_down = (z + 1) % 4, (z + 3) % 4
    dev_prev = (dp, (pp + 7) % 8, tp)
    dev_up, dev_down = (dp, hi * 4 + z_up, tp), (dp, hi * 4 + z_down, tp)
    dev_far = (dp, (1 - hi) * 4 + z, tp)
    dev_far_up, dev_far_down = (dp, (1 - hi) * 4 + z_up, tp), (dp, (1 - hi) * 4 + z_down, tp)
    dev_hop3 = (dp, jnp.where(z == 2, 1 - hi, hi) * 4 + z_up, tp)

    sent = []

    def remote(src, dst, k, dev, arrival=None):
        return pltpu.make_async_remote_copy(
            src_ref=src, dst_ref=dst, send_sem=ssem.at[k], recv_sem=rsem.at[k if arrival is None else arrival],
            device_id=dev, device_id_type=MESH,
        )

    def local(src, dst, k):
        return pltpu.make_async_copy(src, dst, lsem.at[k])

    w_copies = []
    for h in range(2):
        for n, ref in enumerate((kw_ref, vw_ref)):
            c = local(ref.at[:, pl.ds(h * HD, HD)], wg.at[h, j_me, :, pl.ds(n * HD, HD)], W_SEM + 2 * h + n)
            c.start()
            w_copies.append(c)
    hid_copies = []
    for j in range(8):
        c = local(hidden_ref.at[:, pl.ds(j * SHARD, SHARD)], hid.at[:, pl.ds(j * SHARD, SHARD)], HID_SEM + j)
        c.start()
        hid_copies.append(c)
    q_copy = local(query_ref, qs, Q_SEM)
    g_copy = local(grad_ref, gs, G_SEM)
    q_copy.start()
    g_copy.start()

    barrier = pltpu.get_barrier_semaphore()
    for dev in (dev_p, dev_m, dev_y, dev_t, dev_up, dev_down, dev_far, dev_far_up, dev_far_down):
        pl.semaphore_signal(barrier, inc=1, device_id=dev, device_id_type=MESH)
    pl.semaphore_wait(barrier, 9)

    def gather_copy(h, name):
        dev = {"p": dev_p, "m": dev_m, "y": dev_y}[name[0]]
        j = {"p0": j_me, "m0": j_me, "y0": j_me, "p1": j_m, "m1": j_p, "p2": j_q, "m2": j_q, "y2": j_2}[name[:2]]
        rows = pl.ds(0 if name[2] == "a" else HALF, HALF)
        block = wg.at[h, j, rows]
        return remote(block, block, h * PER_HEAD + GATHER.index(name), dev)

    def gather_start(h, *names):
        for name in names:
            c = gather_copy(h, name)
            c.start()
            sent.append(c)

    def gather_wait(h, *names):
        for name in names:
            gather_copy(h, name).wait_recv()

    def project(h, j, first=False):
        columns = pl.ds(pl.multiple_of(j * SHARD, SHARD), SHARD)
        term = jnp.dot(hid[:, columns], wg[h, j], preferred_element_type=jnp.float32)
        if first:
            acc[...] = term
        else:
            acc[...] += term

    def attend(h, b):
        w0 = 128 * max(b - 1, 0)
        window = pl.ds(w0, 256)

        def pair(i, carry):
            c0 = pl.multiple_of((h * GROUP + 2 * i) * HD, 2 * HD)
            rows = pl.ds(b * 128, 128)
            q2 = jnp.concatenate([qs[rows, pl.ds(c0, HD)], qs[rows, pl.ds(c0 + HD, HD)]], axis=0)
            g2 = jnp.concatenate([gs[rows, pl.ds(c0, HD)], gs[rows, pl.ds(c0 + HD, HD)]], axis=0)
            keys = kv[h, window, pl.ds(0, HD)]
            values = kv[h, window, pl.ds(HD, HD)]
            mask = bias[b]
            s = lax.dot_general(keys, q2, NT, preferred_element_type=jnp.float32)
            s = s * (HD ** -0.5) + jnp.concatenate([mask, mask], axis=1)
            top = jnp.max(s, axis=0, keepdims=True)
            e = jnp.exp(s - top)
            p = e * (1.0 / jnp.sum(e, axis=0, keepdims=True))
            low = p.astype(jnp.bfloat16)
            dpr = lax.dot_general(values, g2, NT, preferred_element_type=jnp.float32)
            delta = jnp.sum(low.astype(jnp.float32) * dpr, axis=0, keepdims=True)
            ds = (p * (dpr - delta)).astype(jnp.bfloat16)
            dq = lax.dot_general(ds, keys, TN, preferred_element_type=jnp.float32) * (HD ** -0.5)
            dq = dq.astype(jnp.bfloat16)
            dqs[rows, pl.ds(c0, HD)] = dq[:128]
            dqs[rows, pl.ds(c0 + HD, HD)] = dq[128:]
            gacc[window, pl.ds(0, HD)] += jnp.dot(ds, q2, preferred_element_type=jnp.float32)
            gacc[window, pl.ds(HD, HD)] += jnp.dot(low, g2, preferred_element_type=jnp.float32)
            return carry

        lax.fori_loop(0, GROUP // 2, pair, 0)

    def finish_head(h):
        columns = pl.ds(h * GROUP * HD, GROUP * HD)
        local(dqs.at[:, columns], dq_ref.at[:, columns], DQ_SEM + h).start()
        key_part = gacc[:, pl.ds(0, HD)] * (HD ** -0.5)
        value_part = gacc[:, pl.ds(HD, HD)]
        gkv[h, :, pl.ds(0, HD)] = key_part.astype(jnp.bfloat16)
        gkv[h, :, pl.ds(HD, HD)] = value_part.astype(jnp.bfloat16)
        gkvt[h, pl.ds(0, HD), :] = key_part.T.astype(jnp.bfloat16)
        gkvt[h, pl.ds(HD, HD), :] = value_part.T.astype(jnp.bfloat16)

    targets = (j_2q, j_pq, j_mq, j_2, j_q, j_p, j_m)

    def term(h, j):
        columns = pl.ds(pl.multiple_of(j * SHARD, SHARD), SHARD)
        out = jnp.dot(gkvt[h], hid[:, columns], preferred_element_type=jnp.float32)
        return (out * ((ROWS * 8) ** -0.5)).astype(jnp.bfloat16)

    def terms(h, *slots):
        for n in slots:
            prod[h, n] = term(h, targets[n])

    krows, vrows = pl.ds(0, HD), pl.ds(HD, HD)

    def scatter_copy(h, name):
        src, dst, dev = {
            "y1": (prod.at[h, 0], ry1.at[h], dev_y),
            "p1": (prod.at[h, 1], rp1.at[h], dev_p),
            "m1": (prod.at[h, 2], rm1.at[h], dev_m),
            "p2": (prod.at[h, 3, krows], rp2.at[h], dev_p),
            "m2": (prod.at[h, 3, vrows], rm2.at[h], dev_m),
            "y3": (prod.at[h, 4], ry3.at[h], dev_y),
            "p3k": (prod.at[h, 5, krows], rp3.at[h, krows], dev_p),
            "p3v": (prod.at[h, 5, vrows], rp3.at[h, vrows], dev_p),
            "m3k": (prod.at[h, 6, krows], rm3.at[h, krows], dev_m),
            "m3v": (prod.at[h, 6, vrows], rm3.at[h, vrows], dev_m),
        }[name]
        return remote(src, dst, h * PER_HEAD + len(GATHER) + SCATTER.index(name), dev)

    def scatter_start(h, *names):
        for name in names:
            c = scatter_copy(h, name)
            c.start()
            sent.append(c)

    def scatter_wait(h, *names):
        for name in names:
            scatter_copy(h, name).wait_recv()

    def wide(block):
        return block.astype(jnp.float32)

    def scatter_first(h):
        terms(h, 0, 1, 2)
        scatter_start(h, "y1", "p1", "m1")

    def scatter_rest_terms(h):
        terms(h, 3, 4, 5, 6)
        scatter_start(h, "p3v", "m3k")

    def scatter_second(h):
        scatter_wait(h, "y1")
        prod[h, 3] = (wide(prod[h, 3]) + wide(ry1[h])).astype(jnp.bfloat16)
        scatter_start(h, "p2", "m2")
        scatter_wait(h, "p1", "m1")
        prod[h, 4] = (wide(prod[h, 4]) + wide(rp1[h]) + wide(rm1[h])).astype(jnp.bfloat16)
        scatter_start(h, "y3")

    def scatter_third(h):
        scatter_wait(h, "p2", "m2")
        prod[h, 5, krows] = (wide(prod[h, 5, krows]) + wide(rp2[h])).astype(jnp.bfloat16)
        scatter_start(h, "p3k")
        prod[h, 6, vrows] = (wide(prod[h, 6, vrows]) + wide(rm2[h])).astype(jnp.bfloat16)
        scatter_start(h, "m3v")

    def scatter_last(h):
        own = term(h, j_me)
        scatter_wait(h, "y3", "p3k", "p3v", "m3k", "m3v")
        total = wide(own) + wide(ry3[h]) + wide(rp3[h]) + wide(rm3[h])
        wks[:, pl.ds(h * HD, HD)] = total[:HD].T
        wvs[:, pl.ds(h * HD, HD)] = total[HD:].T

    for c in w_copies[:2]:
        c.wait()
    gather_start(0, "p0a", "m0b", "y0a", "p0b", "m0a", "y0b")
    for c in w_copies[2:]:
        c.wait()
    ends, last = [], jnp.int32(0)
    for k in range(8):
        last = last + len_ref[0, k]
        ends.append(last)
    for b in range(4):
        w0 = 128 * max(b - 1, 0)
        key_at = lax.broadcasted_iota(jnp.int32, (256, 128), 0) + w0
        query_at = lax.broadcasted_iota(jnp.int32, (256, 128), 1) + b * 128
        key_doc = jnp.zeros((256, 128), jnp.int32)
        query_doc = jnp.zeros((256, 128), jnp.int32)
        for end in ends:
            key_doc += (key_at >= end).astype(jnp.int32)
            query_doc += (query_at >= end).astype(jnp.int32)
        bias[b] = jnp.where((key_doc == query_doc) & (key_at <= query_at), 0.0, -1e30)
    for c in hid_copies:
        c.wait()
    project(0, j_me, True)
    gather_wait(0, "p0a", "m0b")
    gather_start(0, "p1a", "m1b")
    gather_wait(0, "y0a")
    gather_start(0, "p2a", "m2a")
    gather_wait(0, "m0a")
    gather_wait(0, "p0b", "y0b")
    gather_start(0, "p2b", "m2b")
    for j in (j_m, j_p, j_q):
        project(0, j)
    gather_wait(0, "p1a")
    gather_start(0, "y2a")
    gather_wait(0, "m1b")
    gather_start(0, "y2b")
    project(0, j_2)
    gather_wait(0, "p2a", "m2a")
    gather_start(1, "p0a", "m0b", "p0b", "m0a")
    gather_wait(0, "y2a")
    gather_start(1, "y0a", "y0b")
    gather_wait(0, "p2b", "m2b")
    project(0, j_pq)
    project(0, j_mq)
    gather_wait(0, "y2b")
    project(0, j_2q)
    kv[0] = acc[...].astype(jnp.bfloat16)
    q_copy.wait()
    g_copy.wait()

    gacc[...] = jnp.zeros_like(gacc)
    attend(0, 0)
    gather_wait(1, "p0a", "m0b")
    gather_start(1, "p1a", "m1b")
    gather_wait(1, "y0a")
    gather_start(1, "p2a", "m2a")
    attend(0, 1)
    gather_wait(1, "m0a")
    gather_wait(1, "p0b", "y0b")
    gather_start(1, "p2b", "m2b")
    attend(0, 2)
    gather_wait(1, "p1a")
    gather_start(1, "y2a")
    gather_wait(1, "m1b")
    gather_start(1, "y2b")
    attend(0, 3)
    finish_head(0)
    terms(0, 0, 1, 2)
    project(1, j_me, True)
    for j in (j_m, j_p, j_q, j_2):
        project(1, j)
    gather_wait(1, "p2a", "m2a", "y2a")
    scatter_start(0, "y1", "p1", "m1")
    terms(0, 3, 4, 5, 6)
    gather_wait(1, "p2b", "m2b")
    project(1, j_pq)
    project(1, j_mq)
    gather_wait(1, "y2b")
    project(1, j_2q)
    kv[1] = acc[...].astype(jnp.bfloat16)
    scatter_start(0, "p3v", "m3k")

    gacc[...] = jnp.zeros_like(gacc)
    attend(1, 0)
    attend(1, 1)
    attend(1, 2)
    attend(1, 3)
    finish_head(1)

    def tp_copy(t):
        return remote(lgs.at[t], lgr.at[t], TP_SEM + t, dev_t)

    def out_tile(t):
        return lg_ref.at[:, pl.ds(pl.multiple_of(t * TILE, TILE), TILE)]

    def pp_copy(t):
        return remote(lgo.at[t], out_tile(t), PP_SEM + t, dev_prev)

    def relay_copy(i, t):
        return remote(lgo.at[t], held.at[i], RELAY_SEM + i, dev_down)

    def pass_copy(i, t):
        return remote(held.at[i], out_tile(t), PASS_SEM + i, dev_far, PP_SEM + t)

    def hop1_copy(i, t):
        return remote(lgo.at[t], hop1.at[i], HOP1_SEM + i, dev_up)

    def hop2_copy(i):
        return remote(hop1.at[i], hop2.at[i], HOP2_SEM + i, dev_up)

    def hop3_copy(i, t):
        return remote(hop2.at[i], out_tile(t), HOP3_SEM + i, dev_hop3, PP_SEM + t)

    def second_hop(i):
        hop1_copy(i, LONG_TILES[i]).wait_recv()
        hop2_copy(i).start()

    def third_hop(i):
        hop2_copy(i).wait_recv()
        hop3_copy(i, LONG_TILES[i]).start()

    def pass_on(i):
        @pl.when(z == 3)
        def _():
            relay_copy(i, RELAY_TILES[i]).wait_recv()
            pass_copy(i, RELAY_TILES[i]).start()

    def send_tile(t):
        is_long = (t == LONG_TILES[0]) | (t == LONG_TILES[1])
        is_relay = (z == 0) & ((t == RELAY_TILES[0]) | (t == RELAY_TILES[1]) | (t == RELAY_TILES[2]))

        @pl.when(is_long)
        def _():
            hop1_copy(t // 2, t).start()

        @pl.when(is_relay)
        def _():
            relay_copy(t // 2, t).start()

        @pl.when(jnp.logical_not(is_long | (z == 0)))
        def _():
            pp_copy(t).start()

    def layer_tile(half, t):
        j = half * 4 + t // 2
        rows = pl.ds(pl.multiple_of((t % 2) * TILE, TILE), TILE)
        return lax.dot_general(gkv[0], wg[0, j, rows], NT, preferred_element_type=jnp.float32) + lax.dot_general(
            gkv[1], wg[1, j, rows], NT, preferred_element_type=jnp.float32
        )

    def layer_step(t, carry):
        @pl.when(t < TILES)
        def _():
            lgs[t] = layer_tile(1 - tp, t).astype(jnp.bfloat16)
            tp_copy(t).start()
            lgo[t] = layer_tile(tp, t).astype(jnp.bfloat16)

        @pl.when(t > 0)
        def _():
            tp_copy(t - 1).wait_recv()
            lgo[t - 1] = (wide(lgo[t - 1]) + wide(lgr[t - 1])).astype(jnp.bfloat16)
            send_tile(t - 1)

        return carry

    lax.fori_loop(0, TILES + 1, layer_step, 0)

    def release():
        @pl.when(z == 0)
        def _():
            relay_copy(1, RELAY_TILES[1]).wait_send()
            for t in DIRECT_TILES:
                pp_copy(t).start()


    scatter_second(0)
    terms(1, 0, 1, 2)
    scatter_start(1, "y1", "p1", "m1")
    scatter_third(0)
    scatter_rest_terms(1)
    second_hop(0)
    pass_on(0)
    scatter_last(0)
    scatter_second(1)
    second_hop(1)
    release()
    pass_on(1)
    scatter_third(1)
    third_hop(0)
    pass_on(2)
    scatter_last(1)
    wk_copy = local(wks, wk_ref, WG_SEM)
    wv_copy = local(wvs, wv_ref, WG_SEM + 1)
    wk_copy.start()
    wv_copy.start()
    third_hop(1)
    for c in sent:
        c.wait_send()
    for t in range(TILES):
        tp_copy(t).wait_send()
    for i, t in enumerate(LONG_TILES):
        hop1_copy(i, t).wait_send()
        hop2_copy(i).wait_send()
        hop3_copy(i, t).wait_send()
    for t in range(TILES):
        if t in LONG_TILES:
            continue
        if t not in RELAY_TILES:
            pp_copy(t).wait_send()
            continue
        i = RELAY_TILES.index(t)

        @pl.when(z == 0)
        def _(i=i, t=t):
            if i != 1:
                relay_copy(i, t).wait_send()

        @pl.when(z != 0)
        def _(t=t):
            pp_copy(t).wait_send()

        @pl.when(z == 3)
        def _(i=i, t=t):
            pass_copy(i, t).wait_send()

    for t in range(TILES):
        pp_copy(t).wait_recv()
    for h in range(2):
        columns = pl.ds(h * GROUP * HD, GROUP * HD)
        local(dqs.at[:, columns], dq_ref.at[:, columns], DQ_SEM + h).wait()
    wk_copy.wait()
    wv_copy.wait()


def body(hidden_in, queries, out_grad, key_weight, value_weight, doc_lengths):
    any_space = pl.BlockSpec(memory_space=pl.ANY)
    bf16, f32 = jnp.bfloat16, jnp.float32
    block = (2, 2 * HD, SHARD)
    outs = pl.pallas_call(
        kernel,
        out_shape=(
            jax.ShapeDtypeStruct((ROWS, 2048), bf16),
            jax.ShapeDtypeStruct((ROWS, WIDTH // 2), bf16),
            jax.ShapeDtypeStruct((SHARD, 2 * HD), f32),
            jax.ShapeDtypeStruct((SHARD, 2 * HD), f32),
        ),
        in_specs=[any_space] * 5 + [pl.BlockSpec(memory_space=pltpu.SMEM)],
        out_specs=(any_space,) * 4,
        scratch_shapes=[
            pltpu.VMEM((ROWS, WIDTH), bf16),
            pltpu.VMEM((ROWS, 2048), bf16),
            pltpu.VMEM((ROWS, 2048), bf16),
            pltpu.VMEM((ROWS, 2048), bf16),
            pltpu.VMEM((2, 8, SHARD, 2 * HD), bf16),
            pltpu.VMEM((2, ROWS, 2 * HD), bf16),
            pltpu.VMEM((ROWS, 2 * HD), f32),
            pltpu.VMEM((4, 256, 128), f32),
            pltpu.VMEM((ROWS, 2 * HD), f32),
            pltpu.VMEM((2, ROWS, 2 * HD), bf16),
            pltpu.VMEM((2, 2 * HD, ROWS), bf16),
            pltpu.VMEM((2, 7, 2 * HD, SHARD), bf16),
            pltpu.VMEM(block, bf16),
            pltpu.VMEM(block, bf16),
            pltpu.VMEM(block, bf16),
            pltpu.VMEM((2, HD, SHARD), bf16),
            pltpu.VMEM((2, HD, SHARD), bf16),
            pltpu.VMEM(block, bf16),
            pltpu.VMEM(block, bf16),
            pltpu.VMEM(block, bf16),
            pltpu.VMEM((TILES, ROWS, TILE), bf16),
            pltpu.VMEM((TILES, ROWS, TILE), bf16),
            pltpu.VMEM((TILES, ROWS, TILE), bf16),
            pltpu.VMEM((2, ROWS, TILE), bf16),
            pltpu.VMEM((2, ROWS, TILE), bf16),
            pltpu.VMEM((3, ROWS, TILE), bf16),
            pltpu.VMEM((SHARD, 2 * HD), f32),
            pltpu.VMEM((SHARD, 2 * HD), f32),
            pltpu.SemaphoreType.DMA((REMOTE_SEMS,)),
            pltpu.SemaphoreType.DMA((REMOTE_SEMS,)),
            pltpu.SemaphoreType.DMA((LOCAL_SEMS,)),
        ],
        compiler_params=pltpu.CompilerParams(
            collective_id=0, has_side_effects=True, vmem_limit_bytes=62 * 1024 * 1024
        ),
        cost_estimate=pl.CostEstimate(flops=18_000_000_000, bytes_accessed=24_000_000, transcendentals=2_100_000),
    )(hidden_in[0], queries[0], out_grad[0], key_weight[0], value_weight[0], doc_lengths[0])
    return tuple(out[None] for out in outs)


def solution(mesh):
    return jax.shard_map(
        body,
        mesh=mesh,
        in_specs=(
            P("pp", "dp", None),
            P("pp", "dp", "tp"),
            P("pp", "dp", "tp"),
            P("pp", "dp", "tp"),
            P("pp", "dp", "tp"),
            P("pp", "dp", None),
        ),
        out_specs=(
            P("pp", "dp", "tp"),
            P("pp", "dp", "tp"),
            P("pp", "dp", "tp"),
            P("pp", "dp", "tp"),
        ),
        check_vma=False,
    )
```

```python
import functools

import jax
import jax.numpy as jnp
from jax import lax
from jax.experimental import pallas as pl
from jax.experimental.pallas import tpu as pltpu
from jax.sharding import PartitionSpec as P

HD = 128
ROWS = 512
WIDTH = 8192
SHARD = 1024
HALF = 512
GROUP = 8
TILE = 512
TILES = 8
MESH = pl.DeviceIdType.MESH
NT = (((1,), (1,)), ((), ()))
TN = (((0,), (0,)), ((), ()))

GATHER = ("p0a", "p0b", "m0a", "m0b", "y0a", "y0b", "p1a", "m1b", "p2a", "p2b", "m2a", "m2b", "y2a", "y2b")
SCATTER = ("p2q", "m2q", "p1k", "p1v", "m1k", "m1v", "p2", "m2", "y3", "p3k", "p3v", "m3k", "m3v")
PER_HEAD = len(GATHER) + len(SCATTER)
TP_SEM = 2 * PER_HEAD
PP_SEM = TP_SEM + TILES
HOP1_SEM = PP_SEM + TILES
HOP2_SEM = HOP1_SEM + 2
HOP3_SEM = HOP2_SEM + 2
RELAY_SEM = HOP3_SEM + 2
PASS_SEM = RELAY_SEM + 3
REMOTE_SEMS = PASS_SEM + 3
LONG_TILES = (1, 3)
RELAY_TILES = (0, 2, 4)
DIRECT_TILES = (5, 6, 7)
HID_SEM, Q_SEM, G_SEM, W_SEM, DQ_SEM, WG_SEM = 0, 8, 9, 10, 14, 16
LOCAL_SEMS = 18


def kernel(
    hidden_ref, query_ref, grad_ref, kw_ref, vw_ref, len_ref,
    dq_ref, lg_ref, wk_ref, wv_ref,
    hid, qs, gs, dqs, wg, kv, acc, bias, gacc, gkv, gkvt, prod,
    rp2q, rm2q, rp1, rm1, rp2, rm2, ry3, rp3, rm3,
    lgs, lgr, lgo, hop1, hop2, held, wks, wvs, ssem, rsem, lsem,
):
    dp, pp, tp = lax.axis_index("dp"), lax.axis_index("pp"), lax.axis_index("tp")
    x, y = dp // 2, dp % 2
    xp, xm, x2, yq = (x + 1) % 4, (x + 3) % 4, (x + 2) % 4, 1 - y
    j_me, j_p, j_m, j_2 = dp, xp * 2 + y, xm * 2 + y, x2 * 2 + y
    j_q, j_pq, j_mq, j_2q = x * 2 + yq, xp * 2 + yq, xm * 2 + yq, x2 * 2 + yq
    dev_p, dev_m, dev_y = (j_p, pp, tp), (j_m, pp, tp), (j_q, pp, tp)
    dev_t = (dp, pp, 1 - tp)
    hi, z = pp // 4, pp % 4
    z_up, z_down = (z + 1) % 4, (z + 3) % 4
    dev_prev = (dp, (pp + 7) % 8, tp)
    dev_up, dev_down = (dp, hi * 4 + z_up, tp), (dp, hi * 4 + z_down, tp)
    dev_far = (dp, (1 - hi) * 4 + z, tp)
    dev_far_up, dev_far_down = (dp, (1 - hi) * 4 + z_up, tp), (dp, (1 - hi) * 4 + z_down, tp)
    dev_hop3 = (dp, jnp.where(z == 2, 1 - hi, hi) * 4 + z_up, tp)

    sent = []

    def remote(src, dst, k, dev, arrival=None):
        return pltpu.make_async_remote_copy(
            src_ref=src, dst_ref=dst, send_sem=ssem.at[k], recv_sem=rsem.at[k if arrival is None else arrival],
            device_id=dev, device_id_type=MESH,
        )

    def local(src, dst, k):
        return pltpu.make_async_copy(src, dst, lsem.at[k])

    w_copies = []
    for h in range(2):
        for n, ref in enumerate((kw_ref, vw_ref)):
            c = local(ref.at[:, pl.ds(h * HD, HD)], wg.at[h, j_me, :, pl.ds(n * HD, HD)], W_SEM + 2 * h + n)
            c.start()
            w_copies.append(c)
    hid_copies = []
    for j in range(8):
        c = local(hidden_ref.at[:, pl.ds(j * SHARD, SHARD)], hid.at[:, pl.ds(j * SHARD, SHARD)], HID_SEM + j)
        c.start()
        hid_copies.append(c)
    q_copy = local(query_ref, qs, Q_SEM)
    g_copy = local(grad_ref, gs, G_SEM)
    q_copy.start()
    g_copy.start()

    barrier = pltpu.get_barrier_semaphore()
    for dev in (dev_p, dev_m, dev_y, dev_t, dev_up, dev_down, dev_far, dev_far_up, dev_far_down):
        pl.semaphore_signal(barrier, inc=1, device_id=dev, device_id_type=MESH)
    pl.semaphore_wait(barrier, 9)

    def gather_copy(h, name):
        dev = {"p": dev_p, "m": dev_m, "y": dev_y}[name[0]]
        j = {"p0": j_me, "m0": j_me, "y0": j_me, "p1": j_m, "m1": j_p, "p2": j_q, "m2": j_q, "y2": j_2}[name[:2]]
        rows = pl.ds(0 if name[2] == "a" else HALF, HALF)
        block = wg.at[h, j, rows]
        return remote(block, block, h * PER_HEAD + GATHER.index(name), dev)

    def gather_start(h, *names):
        for name in names:
            c = gather_copy(h, name)
            c.start()
            sent.append(c)

    def gather_wait(h, *names):
        for name in names:
            gather_copy(h, name).wait_recv()

    def project(h, j, first=False):
        columns = pl.ds(pl.multiple_of(j * SHARD, SHARD), SHARD)
        term = jnp.dot(hid[:, columns], wg[h, j], preferred_element_type=jnp.float32)
        if first:
            acc[...] = term
        else:
            acc[...] += term

    def project_half(h, j, half):
        columns = pl.ds(pl.multiple_of(j * SHARD + half * HALF, HALF), HALF)
        block = wg[h, j, pl.ds(half * HALF, HALF)]
        acc[...] += jnp.dot(hid[:, columns], block, preferred_element_type=jnp.float32)

    def attend(h, b):
        w0 = 128 * max(b - 1, 0)
        window = pl.ds(w0, 256)

        def pair(i, carry):
            c0 = pl.multiple_of((h * GROUP + 2 * i) * HD, 2 * HD)
            rows = pl.ds(b * 128, 128)
            q2 = jnp.concatenate([qs[rows, pl.ds(c0, HD)], qs[rows, pl.ds(c0 + HD, HD)]], axis=0)
            g2 = jnp.concatenate([gs[rows, pl.ds(c0, HD)], gs[rows, pl.ds(c0 + HD, HD)]], axis=0)
            keys = kv[h, window, pl.ds(0, HD)]
            values = kv[h, window, pl.ds(HD, HD)]
            mask = bias[b]
            s = lax.dot_general(keys, q2, NT, preferred_element_type=jnp.float32)
            s = s * (HD ** -0.5) + jnp.concatenate([mask, mask], axis=1)
            top = jnp.max(s, axis=0, keepdims=True)
            e = jnp.exp(s - top)
            p = e * (1.0 / jnp.sum(e, axis=0, keepdims=True))
            low = p.astype(jnp.bfloat16)
            dpr = lax.dot_general(values, g2, NT, preferred_element_type=jnp.float32)
            delta = jnp.sum(low.astype(jnp.float32) * dpr, axis=0, keepdims=True)
            ds = (p * (dpr - delta)).astype(jnp.bfloat16)
            dq = lax.dot_general(ds, keys, TN, preferred_element_type=jnp.float32) * (HD ** -0.5)
            dq = dq.astype(jnp.bfloat16)
            dqs[rows, pl.ds(c0, HD)] = dq[:128]
            dqs[rows, pl.ds(c0 + HD, HD)] = dq[128:]
            gacc[window, pl.ds(0, HD)] += jnp.dot(ds, q2, preferred_element_type=jnp.float32)
            gacc[window, pl.ds(HD, HD)] += jnp.dot(low, g2, preferred_element_type=jnp.float32)
            return carry

        lax.fori_loop(0, GROUP // 2, pair, 0)

    def finish_head(h):
        columns = pl.ds(h * GROUP * HD, GROUP * HD)
        local(dqs.at[:, columns], dq_ref.at[:, columns], DQ_SEM + h).start()
        key_part = gacc[:, pl.ds(0, HD)] * (HD ** -0.5)
        value_part = gacc[:, pl.ds(HD, HD)]
        gkv[h, :, pl.ds(0, HD)] = key_part.astype(jnp.bfloat16)
        gkv[h, :, pl.ds(HD, HD)] = value_part.astype(jnp.bfloat16)
        gkvt[h, pl.ds(0, HD), :] = key_part.T.astype(jnp.bfloat16)
        gkvt[h, pl.ds(HD, HD), :] = value_part.T.astype(jnp.bfloat16)

    targets = (j_2q, j_pq, j_mq, j_2, j_q, j_p, j_m)

    def term(h, j):
        columns = pl.ds(pl.multiple_of(j * SHARD, SHARD), SHARD)
        out = jnp.dot(gkvt[h], hid[:, columns], preferred_element_type=jnp.float32)
        return (out * ((ROWS * 8) ** -0.5)).astype(jnp.bfloat16)

    def terms(h, *slots):
        for n in slots:
            prod[h, n] = term(h, targets[n])

    krows, vrows = pl.ds(0, HD), pl.ds(HD, HD)

    def scatter_copy(h, name):
        src, dst, dev = {
            "p2q": (prod.at[h, 0, krows], rp2q.at[h], dev_p),
            "m2q": (prod.at[h, 0, vrows], rm2q.at[h], dev_m),
            "p1k": (prod.at[h, 1, krows], rp1.at[h, krows], dev_p),
            "p1v": (prod.at[h, 1, vrows], rp1.at[h, vrows], dev_p),
            "m1k": (prod.at[h, 2, krows], rm1.at[h, krows], dev_m),
            "m1v": (prod.at[h, 2, vrows], rm1.at[h, vrows], dev_m),
            "p2": (prod.at[h, 3, krows], rp2.at[h], dev_p),
            "m2": (prod.at[h, 3, vrows], rm2.at[h], dev_m),
            "y3": (prod.at[h, 4], ry3.at[h], dev_y),
            "p3k": (prod.at[h, 5, krows], rp3.at[h, krows], dev_p),
            "p3v": (prod.at[h, 5, vrows], rp3.at[h, vrows], dev_p),
            "m3k": (prod.at[h, 6, krows], rm3.at[h, krows], dev_m),
            "m3v": (prod.at[h, 6, vrows], rm3.at[h, vrows], dev_m),
        }[name]
        return remote(src, dst, h * PER_HEAD + len(GATHER) + SCATTER.index(name), dev)

    def scatter_start(h, *names):
        for name in names:
            c = scatter_copy(h, name)
            c.start()
            sent.append(c)

    def scatter_wait(h, *names):
        for name in names:
            scatter_copy(h, name).wait_recv()

    def wide(block):
        return block.astype(jnp.float32)

    def add(h, n, rows, *arrived):
        total = wide(prod[h, n, rows])
        for block in arrived:
            total = total + wide(block)
        prod[h, n, rows] = total.astype(jnp.bfloat16)

    def scatter_first(h):
        scatter_start(h, "p2q", "m2q", "p1v", "m1k", "p2", "m2")

    def scatter_second(h):
        scatter_wait(h, "p2q", "m2q")
        add(h, 1, krows, rp2q[h])
        scatter_start(h, "p1k")
        add(h, 2, vrows, rm2q[h])
        scatter_start(h, "m1v")
        scatter_wait(h, "p2", "m2")
        add(h, 5, krows, rp2[h])
        scatter_start(h, "p3k")
        add(h, 6, vrows, rm2[h])
        scatter_start(h, "m3v")

    def scatter_third(h):
        scatter_wait(h, "p1k", "p1v", "m1k", "m1v")
        add(h, 4, krows, rp1[h, krows], rm1[h, krows])
        add(h, 4, vrows, rp1[h, vrows], rm1[h, vrows])
        scatter_start(h, "y3")

    def scatter_last(h):
        own = term(h, j_me)
        scatter_wait(h, "y3", "p3k", "p3v", "m3k", "m3v")
        total = wide(own) + wide(ry3[h]) + wide(rp3[h]) + wide(rm3[h])
        wks[:, pl.ds(h * HD, HD)] = total[:HD].T
        wvs[:, pl.ds(h * HD, HD)] = total[HD:].T

    for c in w_copies[:2]:
        c.wait()
    gather_start(0, "p0a", "m0b", "y0a", "p0b", "m0a", "y0b")
    for c in w_copies[2:]:
        c.wait()
    ends, last = [], jnp.int32(0)
    for k in range(8):
        last = last + len_ref[0, k]
        ends.append(last)
    for b in range(4):
        w0 = 128 * max(b - 1, 0)
        key_at = lax.broadcasted_iota(jnp.int32, (256, 128), 0) + w0
        query_at = lax.broadcasted_iota(jnp.int32, (256, 128), 1) + b * 128
        key_doc = jnp.zeros((256, 128), jnp.int32)
        query_doc = jnp.zeros((256, 128), jnp.int32)
        for end in ends:
            key_doc += (key_at >= end).astype(jnp.int32)
            query_doc += (query_at >= end).astype(jnp.int32)
        bias[b] = jnp.where((key_doc == query_doc) & (key_at <= query_at), 0.0, -1e30)
    for c in hid_copies:
        c.wait()
    project(0, j_me, True)
    gather_wait(0, "p0a", "m0b")
    gather_start(0, "p1a", "m1b")
    gather_wait(0, "y0a")
    gather_start(0, "p2a", "m2a")
    gather_wait(0, "m0a")
    gather_wait(0, "p0b", "y0b")
    gather_start(0, "p2b", "m2b")
    for j in (j_m, j_p, j_q):
        project(0, j)
    gather_wait(0, "p1a")
    gather_start(0, "y2a")
    gather_wait(0, "m1b")
    gather_start(0, "y2b")
    project(0, j_2)
    gather_wait(0, "p2a", "m2a")
    gather_start(1, "p0a", "m0b", "p0b", "m0a")
    gather_wait(0, "y2a")
    gather_start(1, "y0a", "y0b")
    gather_wait(0, "p2b", "m2b")
    project(0, j_pq)
    project(0, j_mq)
    gather_wait(0, "y2b")
    project(0, j_2q)
    kv[0] = acc[...].astype(jnp.bfloat16)
    q_copy.wait()
    g_copy.wait()

    gacc[...] = jnp.zeros_like(gacc)
    attend(0, 0)
    gather_wait(1, "p0a", "m0b")
    gather_start(1, "p1a", "m1b")
    gather_wait(1, "y0a")
    gather_start(1, "p2a", "m2a")
    attend(0, 1)
    gather_wait(1, "m0a")
    gather_wait(1, "p0b", "y0b")
    gather_start(1, "p2b", "m2b")
    attend(0, 2)
    gather_wait(1, "p1a")
    gather_start(1, "y2a")
    gather_wait(1, "m1b")
    gather_start(1, "y2b")
    attend(0, 3)
    finish_head(0)
    terms(0, 0, 1, 2, 3)
    project(1, j_me, True)
    for j in (j_m, j_p, j_q, j_2):
        project(1, j)
    terms(0, 4, 5, 6)
    gather_wait(1, "p2a", "m2a", "y2a")
    scatter_first(0)
    scatter_start(0, "p3v", "m3k")
    project_half(1, j_pq, 0)
    project_half(1, j_mq, 0)
    project_half(1, j_2q, 0)
    gather_wait(1, "p2b", "m2b")
    project_half(1, j_pq, 1)
    project_half(1, j_mq, 1)
    gather_wait(1, "y2b")
    project_half(1, j_2q, 1)
    kv[1] = acc[...].astype(jnp.bfloat16)

    gacc[...] = jnp.zeros_like(gacc)
    attend(1, 0)
    attend(1, 1)
    attend(1, 2)
    attend(1, 3)
    finish_head(1)

    def tp_copy(t):
        return remote(lgs.at[t], lgr.at[t], TP_SEM + t, dev_t)

    def out_tile(t):
        return lg_ref.at[:, pl.ds(pl.multiple_of(t * TILE, TILE), TILE)]

    def pp_copy(t):
        return remote(lgo.at[t], out_tile(t), PP_SEM + t, dev_prev)

    def relay_copy(i, t):
        return remote(lgo.at[t], held.at[i], RELAY_SEM + i, dev_down)

    def pass_copy(i, t):
        return remote(held.at[i], out_tile(t), PASS_SEM + i, dev_far, PP_SEM + t)

    def hop1_copy(i, t):
        return remote(lgo.at[t], hop1.at[i], HOP1_SEM + i, dev_up)

    def hop2_copy(i):
        return remote(hop1.at[i], hop2.at[i], HOP2_SEM + i, dev_up)

    def hop3_copy(i, t):
        return remote(hop2.at[i], out_tile(t), HOP3_SEM + i, dev_hop3, PP_SEM + t)

    def second_hop(i):
        hop1_copy(i, LONG_TILES[i]).wait_recv()
        hop2_copy(i).start()

    def third_hop(i):
        hop2_copy(i).wait_recv()
        hop3_copy(i, LONG_TILES[i]).start()

    def pass_on(i):
        @pl.when(z == 3)
        def _():
            relay_copy(i, RELAY_TILES[i]).wait_recv()
            pass_copy(i, RELAY_TILES[i]).start()

    def send_tile(t):
        is_long = (t == LONG_TILES[0]) | (t == LONG_TILES[1])
        is_relay = (z == 0) & ((t == RELAY_TILES[0]) | (t == RELAY_TILES[1]) | (t == RELAY_TILES[2]))

        @pl.when(is_long)
        def _():
            hop1_copy(t // 2, t).start()

        @pl.when(is_relay)
        def _():
            relay_copy(t // 2, t).start()

        @pl.when(jnp.logical_not(is_long) & ((z != 0) | (t == DIRECT_TILES[0])))
        def _():
            pp_copy(t).start()

    def layer_tile(half, t):
        j = half * 4 + t // 2
        rows = pl.ds(pl.multiple_of((t % 2) * TILE, TILE), TILE)
        return lax.dot_general(gkv[0], wg[0, j, rows], NT, preferred_element_type=jnp.float32) + lax.dot_general(
            gkv[1], wg[1, j, rows], NT, preferred_element_type=jnp.float32
        )

    def layer_step(t, carry):
        @pl.when(t < TILES)
        def _():
            lgs[t] = layer_tile(1 - tp, t).astype(jnp.bfloat16)
            tp_copy(t).start()
            lgo[t] = layer_tile(tp, t).astype(jnp.bfloat16)

        @pl.when(t > 0)
        def _():
            tp_copy(t - 1).wait_recv()
            lgo[t - 1] = (wide(lgo[t - 1]) + wide(lgr[t - 1])).astype(jnp.bfloat16)
            send_tile(t - 1)

        return carry

    lax.fori_loop(0, TILES + 1, layer_step, 0)

    def release():
        @pl.when(z == 0)
        def _():
            relay_copy(1, RELAY_TILES[1]).wait_send()
            for t in DIRECT_TILES[1:]:
                pp_copy(t).start()


    scatter_second(0)
    terms(1, 0, 1, 2, 3)
    scatter_first(1)
    terms(1, 4, 5, 6)
    scatter_start(1, "p3v", "m3k")
    second_hop(0)
    scatter_third(0)
    pass_on(0)
    second_hop(1)
    scatter_last(0)
    scatter_second(1)
    pass_on(1)
    release()
    third_hop(0)
    pass_on(2)
    scatter_third(1)
    third_hop(1)
    scatter_last(1)
    wk_copy = local(wks, wk_ref, WG_SEM)
    wv_copy = local(wvs, wv_ref, WG_SEM + 1)
    wk_copy.start()
    wv_copy.start()
    for c in sent:
        c.wait_send()
    for t in range(TILES):
        tp_copy(t).wait_send()
    for i, t in enumerate(LONG_TILES):
        hop1_copy(i, t).wait_send()
        hop2_copy(i).wait_send()
        hop3_copy(i, t).wait_send()
    for t in range(TILES):
        if t in LONG_TILES:
            continue
        if t not in RELAY_TILES:
            pp_copy(t).wait_send()
            continue
        i = RELAY_TILES.index(t)

        @pl.when(z == 0)
        def _(i=i, t=t):
            if i != 1:
                relay_copy(i, t).wait_send()

        @pl.when(z != 0)
        def _(t=t):
            pp_copy(t).wait_send()

        @pl.when(z == 3)
        def _(i=i, t=t):
            pass_copy(i, t).wait_send()

    for t in range(TILES):
        pp_copy(t).wait_recv()
    for h in range(2):
        columns = pl.ds(h * GROUP * HD, GROUP * HD)
        local(dqs.at[:, columns], dq_ref.at[:, columns], DQ_SEM + h).wait()
    wk_copy.wait()
    wv_copy.wait()


def body(hidden_in, queries, out_grad, key_weight, value_weight, doc_lengths):
    any_space = pl.BlockSpec(memory_space=pl.ANY)
    bf16, f32 = jnp.bfloat16, jnp.float32
    block = (2, 2 * HD, SHARD)
    outs = pl.pallas_call(
        kernel,
        out_shape=(
            jax.ShapeDtypeStruct((ROWS, 2048), bf16),
            jax.ShapeDtypeStruct((ROWS, WIDTH // 2), bf16),
            jax.ShapeDtypeStruct((SHARD, 2 * HD), f32),
            jax.ShapeDtypeStruct((SHARD, 2 * HD), f32),
        ),
        in_specs=[any_space] * 5 + [pl.BlockSpec(memory_space=pltpu.SMEM)],
        out_specs=(any_space,) * 4,
        scratch_shapes=[
            pltpu.VMEM((ROWS, WIDTH), bf16),
            pltpu.VMEM((ROWS, 2048), bf16),
            pltpu.VMEM((ROWS, 2048), bf16),
            pltpu.VMEM((ROWS, 2048), bf16),
            pltpu.VMEM((2, 8, SHARD, 2 * HD), bf16),
            pltpu.VMEM((2, ROWS, 2 * HD), bf16),
            pltpu.VMEM((ROWS, 2 * HD), f32),
            pltpu.VMEM((4, 256, 128), f32),
            pltpu.VMEM((ROWS, 2 * HD), f32),
            pltpu.VMEM((2, ROWS, 2 * HD), bf16),
            pltpu.VMEM((2, 2 * HD, ROWS), bf16),
            pltpu.VMEM((2, 7, 2 * HD, SHARD), bf16),
            pltpu.VMEM((2, HD, SHARD), bf16),
            pltpu.VMEM((2, HD, SHARD), bf16),
            pltpu.VMEM(block, bf16),
            pltpu.VMEM(block, bf16),
            pltpu.VMEM((2, HD, SHARD), bf16),
            pltpu.VMEM((2, HD, SHARD), bf16),
            pltpu.VMEM(block, bf16),
            pltpu.VMEM(block, bf16),
            pltpu.VMEM(block, bf16),
            pltpu.VMEM((TILES, ROWS, TILE), bf16),
            pltpu.VMEM((TILES, ROWS, TILE), bf16),
            pltpu.VMEM((TILES, ROWS, TILE), bf16),
            pltpu.VMEM((2, ROWS, TILE), bf16),
            pltpu.VMEM((2, ROWS, TILE), bf16),
            pltpu.VMEM((3, ROWS, TILE), bf16),
            pltpu.VMEM((SHARD, 2 * HD), f32),
            pltpu.VMEM((SHARD, 2 * HD), f32),
            pltpu.SemaphoreType.DMA((REMOTE_SEMS,)),
            pltpu.SemaphoreType.DMA((REMOTE_SEMS,)),
            pltpu.SemaphoreType.DMA((LOCAL_SEMS,)),
        ],
        compiler_params=pltpu.CompilerParams(
            collective_id=0, has_side_effects=True, vmem_limit_bytes=62 * 1024 * 1024
        ),
        cost_estimate=pl.CostEstimate(flops=18_000_000_000, bytes_accessed=24_000_000, transcendentals=2_100_000),
    )(hidden_in[0], queries[0], out_grad[0], key_weight[0], value_weight[0], doc_lengths[0])
    return tuple(out[None] for out in outs)


def solution(mesh):
    return jax.shard_map(
        body,
        mesh=mesh,
        in_specs=(
            P("pp", "dp", None),
            P("pp", "dp", "tp"),
            P("pp", "dp", "tp"),
            P("pp", "dp", "tp"),
            P("pp", "dp", "tp"),
            P("pp", "dp", None),
        ),
        out_specs=(
            P("pp", "dp", "tp"),
            P("pp", "dp", "tp"),
            P("pp", "dp", "tp"),
            P("pp", "dp", "tp"),
        ),
        check_vma=False,
    )
```

```python
import functools

import jax
import jax.numpy as jnp
from jax import lax
from jax.experimental import pallas as pl
from jax.experimental.pallas import tpu as pltpu
from jax.sharding import PartitionSpec as P

HD = 128
ROWS = 512
WIDTH = 8192
SHARD = 1024
HALF = 512
GROUP = 8
TILE = 512
TILES = 8
MESH = pl.DeviceIdType.MESH
NT = (((1,), (1,)), ((), ()))
TN = (((0,), (0,)), ((), ()))

GATHER = ("p0a", "p0b", "m0a", "m0b", "y0a", "y0b", "p1a", "m1b", "p2a", "p2b", "m2a", "m2b", "y2a", "y2b")
SCATTER = ("p2q", "m2q", "p1k", "p1v", "m1k", "m1v", "p2", "m2", "y3", "p3k", "p3v", "m3k", "m3v")
PER_HEAD = len(GATHER) + len(SCATTER)
TP_SEM = 2 * PER_HEAD
PP_SEM = TP_SEM + TILES
HOP1_SEM = PP_SEM + TILES
HOP2_SEM = HOP1_SEM + 2
HOP3_SEM = HOP2_SEM + 2
RELAY_SEM = HOP3_SEM + 2
PASS_SEM = RELAY_SEM + 3
REMOTE_SEMS = PASS_SEM + 3
LONG_TILES = (1, 3)
RELAY_TILES = (0, 2, 4)
DIRECT_TILES = (5, 6, 7)
HID_SEM, Q_SEM, G_SEM, W_SEM, DQ_SEM, WG_SEM = 0, 8, 9, 10, 14, 16
LOCAL_SEMS = 18


def kernel(
    hidden_ref, query_ref, grad_ref, kw_ref, vw_ref, len_ref,
    dq_ref, lg_ref, wk_ref, wv_ref,
    hid, qs, gs, wg, kv, acc, bias, gacc, gkv, gkvt, prod,
    rp2q, rm2q, rp1, rm1, rp2, rm2, ry3, rp3, rm3,
    lgs, lgr, lgo, hop1, hop2, held, ssem, rsem, lsem,
):
    dp, pp, tp = lax.axis_index("dp"), lax.axis_index("pp"), lax.axis_index("tp")
    x, y = dp // 2, dp % 2
    xp, xm, x2, yq = (x + 1) % 4, (x + 3) % 4, (x + 2) % 4, 1 - y
    j_me, j_p, j_m, j_2 = dp, xp * 2 + y, xm * 2 + y, x2 * 2 + y
    j_q, j_pq, j_mq, j_2q = x * 2 + yq, xp * 2 + yq, xm * 2 + yq, x2 * 2 + yq
    dev_p, dev_m, dev_y = (j_p, pp, tp), (j_m, pp, tp), (j_q, pp, tp)
    dev_t = (dp, pp, 1 - tp)
    hi, z = pp // 4, pp % 4
    z_up, z_down = (z + 1) % 4, (z + 3) % 4
    dev_prev = (dp, (pp + 7) % 8, tp)
    dev_up, dev_down = (dp, hi * 4 + z_up, tp), (dp, hi * 4 + z_down, tp)
    dev_far = (dp, (1 - hi) * 4 + z, tp)
    dev_far_up, dev_far_down = (dp, (1 - hi) * 4 + z_up, tp), (dp, (1 - hi) * 4 + z_down, tp)
    dev_hop3 = (dp, jnp.where(z == 2, 1 - hi, hi) * 4 + z_up, tp)

    sent = []

    def remote(src, dst, k, dev, arrival=None):
        return pltpu.make_async_remote_copy(
            src_ref=src, dst_ref=dst, send_sem=ssem.at[k], recv_sem=rsem.at[k if arrival is None else arrival],
            device_id=dev, device_id_type=MESH,
        )

    def local(src, dst, k):
        return pltpu.make_async_copy(src, dst, lsem.at[k])

    w_copies = []
    for h in range(2):
        for n, ref in enumerate((kw_ref, vw_ref)):
            c = local(ref.at[:, pl.ds(h * HD, HD)], wg.at[h, j_me, :, pl.ds(n * HD, HD)], W_SEM + 2 * h + n)
            c.start()
            w_copies.append(c)
    hid_copies = []
    for j in range(8):
        c = local(hidden_ref.at[:, pl.ds(j * SHARD, SHARD)], hid.at[:, pl.ds(j * SHARD, SHARD)], HID_SEM + j)
        c.start()
        hid_copies.append(c)
    q_copy = local(query_ref, qs, Q_SEM)
    g_copy = local(grad_ref, gs, G_SEM)
    q_copy.start()
    g_copy.start()

    barrier = pltpu.get_barrier_semaphore()
    for dev in (dev_p, dev_m, dev_y, dev_t, dev_up, dev_down, dev_far, dev_far_up, dev_far_down):
        pl.semaphore_signal(barrier, inc=1, device_id=dev, device_id_type=MESH)
    pl.semaphore_wait(barrier, 9)

    def gather_copy(h, name):
        dev = {"p": dev_p, "m": dev_m, "y": dev_y}[name[0]]
        j = {"p0": j_me, "m0": j_me, "y0": j_me, "p1": j_m, "m1": j_p, "p2": j_q, "m2": j_q, "y2": j_2}[name[:2]]
        rows = pl.ds(0 if name[2] == "a" else HALF, HALF)
        block = wg.at[h, j, rows]
        return remote(block, block, h * PER_HEAD + GATHER.index(name), dev)

    def gather_start(h, *names):
        for name in names:
            c = gather_copy(h, name)
            c.start()
            sent.append(c)

    def gather_wait(h, *names):
        for name in names:
            gather_copy(h, name).wait_recv()

    def project(h, j, first=False):
        columns = pl.ds(pl.multiple_of(j * SHARD, SHARD), SHARD)
        term = jnp.dot(hid[:, columns], wg[h, j], preferred_element_type=jnp.float32)
        if first:
            acc[...] = term
        else:
            acc[...] += term

    def project_half(h, j, half):
        columns = pl.ds(pl.multiple_of(j * SHARD + half * HALF, HALF), HALF)
        block = wg[h, j, pl.ds(half * HALF, HALF)]
        acc[...] += jnp.dot(hid[:, columns], block, preferred_element_type=jnp.float32)

    def attend(h, b):
        w0 = 128 * max(b - 1, 0)
        window = pl.ds(w0, 256)

        def pair(i, carry):
            c0 = pl.multiple_of((h * GROUP + 2 * i) * HD, 2 * HD)
            rows = pl.ds(b * 128, 128)
            q2 = jnp.concatenate([qs[rows, pl.ds(c0, HD)], qs[rows, pl.ds(c0 + HD, HD)]], axis=0)
            g2 = jnp.concatenate([gs[rows, pl.ds(c0, HD)], gs[rows, pl.ds(c0 + HD, HD)]], axis=0)
            keys = kv[h, window, pl.ds(0, HD)]
            values = kv[h, window, pl.ds(HD, HD)]
            mask = bias[b]
            s = lax.dot_general(keys, q2, NT, preferred_element_type=jnp.float32)
            s = s * (HD ** -0.5) + jnp.concatenate([mask, mask], axis=1)
            top = jnp.max(s, axis=0, keepdims=True)
            e = jnp.exp(s - top)
            p = e * (1.0 / jnp.sum(e, axis=0, keepdims=True))
            low = p.astype(jnp.bfloat16)
            dpr = lax.dot_general(values, g2, NT, preferred_element_type=jnp.float32)
            delta = jnp.sum(low.astype(jnp.float32) * dpr, axis=0, keepdims=True)
            ds = (p * (dpr - delta)).astype(jnp.bfloat16)
            dq = lax.dot_general(ds, keys, TN, preferred_element_type=jnp.float32) * (HD ** -0.5)
            dq = dq.astype(jnp.bfloat16)
            dq_ref[rows, pl.ds(c0, HD)] = dq[:128]
            dq_ref[rows, pl.ds(c0 + HD, HD)] = dq[128:]
            gacc[window, pl.ds(0, HD)] += jnp.dot(ds, q2, preferred_element_type=jnp.float32)
            gacc[window, pl.ds(HD, HD)] += jnp.dot(low, g2, preferred_element_type=jnp.float32)
            return carry

        lax.fori_loop(0, GROUP // 2, pair, 0)

    def finish_head(h):
        columns = pl.ds(h * GROUP * HD, GROUP * HD)
        key_part = gacc[:, pl.ds(0, HD)] * (HD ** -0.5)
        value_part = gacc[:, pl.ds(HD, HD)]
        gkv[h, :, pl.ds(0, HD)] = key_part.astype(jnp.bfloat16)
        gkv[h, :, pl.ds(HD, HD)] = value_part.astype(jnp.bfloat16)
        gkvt[h, pl.ds(0, HD), :] = key_part.T.astype(jnp.bfloat16)
        gkvt[h, pl.ds(HD, HD), :] = value_part.T.astype(jnp.bfloat16)

    targets = (j_2q, j_pq, j_mq, j_2, j_q, j_p, j_m)

    def term(h, j):
        columns = pl.ds(pl.multiple_of(j * SHARD, SHARD), SHARD)
        out = jnp.dot(gkvt[h], hid[:, columns], preferred_element_type=jnp.float32)
        return (out * ((ROWS * 8) ** -0.5)).astype(jnp.bfloat16)

    def terms(h, *slots):
        for n in slots:
            prod[h, n] = term(h, targets[n])

    krows, vrows = pl.ds(0, HD), pl.ds(HD, HD)

    def scatter_copy(h, name):
        src, dst, dev = {
            "p2q": (prod.at[h, 0, krows], rp2q.at[h], dev_p),
            "m2q": (prod.at[h, 0, vrows], rm2q.at[h], dev_m),
            "p1k": (prod.at[h, 1, krows], rp1.at[h, krows], dev_p),
            "p1v": (prod.at[h, 1, vrows], rp1.at[h, vrows], dev_p),
            "m1k": (prod.at[h, 2, krows], rm1.at[h, krows], dev_m),
            "m1v": (prod.at[h, 2, vrows], rm1.at[h, vrows], dev_m),
            "p2": (prod.at[h, 3, krows], rp2.at[h], dev_p),
            "m2": (prod.at[h, 3, vrows], rm2.at[h], dev_m),
            "y3": (prod.at[h, 4], ry3.at[h], dev_y),
            "p3k": (prod.at[h, 5, krows], rp3.at[h, krows], dev_p),
            "p3v": (prod.at[h, 5, vrows], rp3.at[h, vrows], dev_p),
            "m3k": (prod.at[h, 6, krows], rm3.at[h, krows], dev_m),
            "m3v": (prod.at[h, 6, vrows], rm3.at[h, vrows], dev_m),
        }[name]
        return remote(src, dst, h * PER_HEAD + len(GATHER) + SCATTER.index(name), dev)

    def scatter_start(h, *names):
        for name in names:
            c = scatter_copy(h, name)
            c.start()
            sent.append(c)

    def scatter_wait(h, *names):
        for name in names:
            scatter_copy(h, name).wait_recv()

    def wide(block):
        return block.astype(jnp.float32)

    def add(h, n, rows, *arrived):
        total = wide(prod[h, n, rows])
        for block in arrived:
            total = total + wide(block)
        prod[h, n, rows] = total.astype(jnp.bfloat16)

    def scatter_first(h):
        scatter_start(h, "p2q", "m2q", "p1v", "m1k", "p2", "m2")

    def scatter_second(h):
        scatter_wait(h, "p2q", "m2q")
        add(h, 1, krows, rp2q[h])
        scatter_start(h, "p1k")
        add(h, 2, vrows, rm2q[h])
        scatter_start(h, "m1v")
        scatter_wait(h, "p2", "m2")
        add(h, 5, krows, rp2[h])
        scatter_start(h, "p3k")
        add(h, 6, vrows, rm2[h])
        scatter_start(h, "m3v")

    def scatter_third(h):
        scatter_wait(h, "p1k", "p1v", "m1k", "m1v")
        add(h, 4, krows, rp1[h, krows], rm1[h, krows])
        add(h, 4, vrows, rp1[h, vrows], rm1[h, vrows])
        scatter_start(h, "y3")

    def scatter_last(h):
        own = term(h, j_me)
        scatter_wait(h, "y3", "p3k", "p3v", "m3k", "m3v")
        total = wide(own) + wide(ry3[h]) + wide(rp3[h]) + wide(rm3[h])
        wk_ref[:, pl.ds(h * HD, HD)] = total[:HD].T
        wv_ref[:, pl.ds(h * HD, HD)] = total[HD:].T

    for c in w_copies[:2]:
        c.wait()
    gather_start(0, "p0a", "m0b", "y0a", "p0b", "m0a", "y0b")
    for c in w_copies[2:]:
        c.wait()
    ends, last = [], jnp.int32(0)
    for k in range(8):
        last = last + len_ref[0, k]
        ends.append(last)
    for b in range(4):
        w0 = 128 * max(b - 1, 0)
        key_at = lax.broadcasted_iota(jnp.int32, (256, 128), 0) + w0
        query_at = lax.broadcasted_iota(jnp.int32, (256, 128), 1) + b * 128
        key_doc = jnp.zeros((256, 128), jnp.int32)
        query_doc = jnp.zeros((256, 128), jnp.int32)
        for end in ends:
            key_doc += (key_at >= end).astype(jnp.int32)
            query_doc += (query_at >= end).astype(jnp.int32)
        bias[b] = jnp.where((key_doc == query_doc) & (key_at <= query_at), 0.0, -1e30)
    for c in hid_copies:
        c.wait()
    project(0, j_me, True)
    gather_wait(0, "p0a", "m0b")
    gather_start(0, "p1a", "m1b")
    gather_wait(0, "y0a")
    gather_start(0, "p2a", "m2a")
    gather_wait(0, "m0a")
    gather_wait(0, "p0b", "y0b")
    gather_start(0, "p2b", "m2b")
    for j in (j_m, j_p, j_q):
        project(0, j)
    gather_wait(0, "p1a")
    gather_start(0, "y2a")
    gather_wait(0, "m1b")
    gather_start(0, "y2b")
    project(0, j_2)
    gather_wait(0, "p2a", "m2a")
    gather_start(1, "p0a", "m0b", "p0b", "m0a")
    gather_wait(0, "y2a")
    gather_start(1, "y0a", "y0b")
    gather_wait(0, "p2b", "m2b")
    project(0, j_pq)
    project(0, j_mq)
    gather_wait(0, "y2b")
    project(0, j_2q)
    kv[0] = acc[...].astype(jnp.bfloat16)
    q_copy.wait()
    g_copy.wait()

    gacc[...] = jnp.zeros_like(gacc)
    attend(0, 0)
    gather_wait(1, "p0a", "m0b")
    gather_start(1, "p1a", "m1b")
    gather_wait(1, "y0a")
    gather_start(1, "p2a", "m2a")
    attend(0, 1)
    gather_wait(1, "m0a")
    gather_wait(1, "p0b", "y0b")
    gather_start(1, "p2b", "m2b")
    attend(0, 2)
    gather_wait(1, "p1a")
    gather_start(1, "y2a")
    gather_wait(1, "m1b")
    gather_start(1, "y2b")
    attend(0, 3)
    finish_head(0)
    terms(0, 0, 1, 2, 3)
    project(1, j_me, True)
    for j in (j_m, j_p, j_q, j_2):
        project(1, j)
    terms(0, 4, 5, 6)
    gather_wait(1, "p2a", "m2a", "y2a")
    scatter_first(0)
    scatter_start(0, "p3v", "m3k")
    project_half(1, j_pq, 0)
    project_half(1, j_mq, 0)
    project_half(1, j_2q, 0)
    gather_wait(1, "p2b", "m2b")
    project_half(1, j_pq, 1)
    project_half(1, j_mq, 1)
    gather_wait(1, "y2b")
    project_half(1, j_2q, 1)
    kv[1] = acc[...].astype(jnp.bfloat16)

    gacc[...] = jnp.zeros_like(gacc)
    attend(1, 0)
    attend(1, 1)
    attend(1, 2)
    attend(1, 3)
    finish_head(1)

    def tp_copy(t):
        return remote(lgs.at[t], lgr.at[t], TP_SEM + t, dev_t)

    def out_tile(t):
        return lg_ref.at[:, pl.ds(pl.multiple_of(t * TILE, TILE), TILE)]

    def pp_copy(t):
        return remote(lgo.at[t], out_tile(t), PP_SEM + t, dev_prev)

    def relay_copy(i, t):
        return remote(lgo.at[t], held.at[i], RELAY_SEM + i, dev_down)

    def pass_copy(i, t):
        return remote(held.at[i], out_tile(t), PASS_SEM + i, dev_far, PP_SEM + t)

    def hop1_copy(i, t):
        return remote(lgo.at[t], hop1.at[i], HOP1_SEM + i, dev_up)

    def hop2_copy(i):
        return remote(hop1.at[i], hop2.at[i], HOP2_SEM + i, dev_up)

    def hop3_copy(i, t):
        return remote(hop2.at[i], out_tile(t), HOP3_SEM + i, dev_hop3, PP_SEM + t)

    def second_hop(i):
        hop1_copy(i, LONG_TILES[i]).wait_recv()
        hop2_copy(i).start()

    def third_hop(i):
        hop2_copy(i).wait_recv()
        hop3_copy(i, LONG_TILES[i]).start()

    def pass_on(i):
        @pl.when(z == 3)
        def _():
            relay_copy(i, RELAY_TILES[i]).wait_recv()
            pass_copy(i, RELAY_TILES[i]).start()

    def send_tile(t):
        is_long = (t == LONG_TILES[0]) | (t == LONG_TILES[1])
        is_relay = (z == 0) & ((t == RELAY_TILES[0]) | (t == RELAY_TILES[1]) | (t == RELAY_TILES[2]))

        @pl.when(is_long)
        def _():
            hop1_copy(t // 2, t).start()

        @pl.when(is_relay)
        def _():
            relay_copy(t // 2, t).start()

        @pl.when(jnp.logical_not(is_long) & ((z != 0) | (t == DIRECT_TILES[0])))
        def _():
            pp_copy(t).start()

    def layer_tile(half, t):
        j = half * 4 + t // 2
        rows = pl.ds(pl.multiple_of((t % 2) * TILE, TILE), TILE)
        return lax.dot_general(gkv[0], wg[0, j, rows], NT, preferred_element_type=jnp.float32) + lax.dot_general(
            gkv[1], wg[1, j, rows], NT, preferred_element_type=jnp.float32
        )

    def layer_step(t, carry):
        @pl.when(t < TILES)
        def _():
            lgs[t] = layer_tile(1 - tp, t).astype(jnp.bfloat16)
            tp_copy(t).start()
            lgo[t] = layer_tile(tp, t).astype(jnp.bfloat16)

        @pl.when(t > 0)
        def _():
            tp_copy(t - 1).wait_recv()
            lgo[t - 1] = (wide(lgo[t - 1]) + wide(lgr[t - 1])).astype(jnp.bfloat16)
            send_tile(t - 1)

        return carry

    lax.fori_loop(0, TILES + 1, layer_step, 0)

    def release(t, wait):
        @pl.when(z == 0)
        def _():
            if wait:
                relay_copy(1, RELAY_TILES[1]).wait_send()
            pp_copy(t).start()

    scatter_second(0)
    terms(1, 0, 1, 2, 3)
    scatter_first(1)
    terms(1, 4, 5, 6)
    scatter_start(1, "p3v", "m3k")
    second_hop(0)
    scatter_third(0)
    pass_on(0)
    second_hop(1)
    scatter_last(0)
    scatter_second(1)
    release(DIRECT_TILES[1], True)
    pass_on(1)
    third_hop(0)
    scatter_third(1)
    release(DIRECT_TILES[2], False)
    third_hop(1)
    pass_on(2)
    scatter_last(1)
    for c in sent:
        c.wait_send()
    for t in range(TILES):
        tp_copy(t).wait_send()
    for i, t in enumerate(LONG_TILES):
        hop1_copy(i, t).wait_send()
        hop2_copy(i).wait_send()
        hop3_copy(i, t).wait_send()
    for t in range(TILES):
        if t in LONG_TILES:
            continue
        if t not in RELAY_TILES:
            pp_copy(t).wait_send()
            continue
        i = RELAY_TILES.index(t)

        @pl.when(z == 0)
        def _(i=i, t=t):
            if i != 1:
                relay_copy(i, t).wait_send()

        @pl.when(z != 0)
        def _(t=t):
            pp_copy(t).wait_send()

        @pl.when(z == 3)
        def _(i=i, t=t):
            pass_copy(i, t).wait_send()

    for t in range(TILES):
        pp_copy(t).wait_recv()


def body(hidden_in, queries, out_grad, key_weight, value_weight, doc_lengths):
    any_space = pl.BlockSpec(memory_space=pl.ANY)
    vmem_space = pl.BlockSpec(memory_space=pltpu.VMEM)
    bf16, f32 = jnp.bfloat16, jnp.float32
    block = (2, 2 * HD, SHARD)
    outs = pl.pallas_call(
        kernel,
        out_shape=(
            pltpu.VMEM((ROWS, 2048), bf16),
            jax.ShapeDtypeStruct((ROWS, WIDTH // 2), bf16),
            pltpu.VMEM((SHARD, 2 * HD), f32),
            pltpu.VMEM((SHARD, 2 * HD), f32),
        ),
        in_specs=[any_space] * 5 + [pl.BlockSpec(memory_space=pltpu.SMEM)],
        out_specs=(vmem_space, any_space, vmem_space, vmem_space),
        scratch_shapes=[
            pltpu.VMEM((ROWS, WIDTH), bf16),
            pltpu.VMEM((ROWS, 2048), bf16),
            pltpu.VMEM((ROWS, 2048), bf16),
            pltpu.VMEM((2, 8, SHARD, 2 * HD), bf16),
            pltpu.VMEM((2, ROWS, 2 * HD), bf16),
            pltpu.VMEM((ROWS, 2 * HD), f32),
            pltpu.VMEM((4, 256, 128), f32),
            pltpu.VMEM((ROWS, 2 * HD), f32),
            pltpu.VMEM((2, ROWS, 2 * HD), bf16),
            pltpu.VMEM((2, 2 * HD, ROWS), bf16),
            pltpu.VMEM((2, 7, 2 * HD, SHARD), bf16),
            pltpu.VMEM((2, HD, SHARD), bf16),
            pltpu.VMEM((2, HD, SHARD), bf16),
            pltpu.VMEM(block, bf16),
            pltpu.VMEM(block, bf16),
            pltpu.VMEM((2, HD, SHARD), bf16),
            pltpu.VMEM((2, HD, SHARD), bf16),
            pltpu.VMEM(block, bf16),
            pltpu.VMEM(block, bf16),
            pltpu.VMEM(block, bf16),
            pltpu.VMEM((TILES, ROWS, TILE), bf16),
            pltpu.VMEM((TILES, ROWS, TILE), bf16),
            pltpu.VMEM((TILES, ROWS, TILE), bf16),
            pltpu.VMEM((2, ROWS, TILE), bf16),
            pltpu.VMEM((2, ROWS, TILE), bf16),
            pltpu.VMEM((3, ROWS, TILE), bf16),
            pltpu.SemaphoreType.DMA((REMOTE_SEMS,)),
            pltpu.SemaphoreType.DMA((REMOTE_SEMS,)),
            pltpu.SemaphoreType.DMA((LOCAL_SEMS,)),
        ],
        compiler_params=pltpu.CompilerParams(
            collective_id=0, has_side_effects=True, vmem_limit_bytes=56 * 1024 * 1024
        ),
        cost_estimate=pl.CostEstimate(flops=18_000_000_000, bytes_accessed=24_000_000, transcendentals=2_100_000),
    )(hidden_in[0], queries[0], out_grad[0], key_weight[0], value_weight[0], doc_lengths[0])
    return tuple(out[None] for out in outs)


def solution(mesh):
    return jax.shard_map(
        body,
        mesh=mesh,
        in_specs=(
            P("pp", "dp", None),
            P("pp", "dp", "tp"),
            P("pp", "dp", "tp"),
            P("pp", "dp", "tp"),
            P("pp", "dp", "tp"),
            P("pp", "dp", None),
        ),
        out_specs=(
            P("pp", "dp", "tp"),
            P("pp", "dp", "tp"),
            P("pp", "dp", "tp"),
            P("pp", "dp", "tp"),
        ),
        check_vma=False,
    )
```

```python
import functools

import jax
import jax.numpy as jnp
from jax import lax
from jax.experimental import pallas as pl
from jax.experimental.pallas import tpu as pltpu
from jax.sharding import PartitionSpec as P

HD = 128
ROWS = 512
WIDTH = 8192
SHARD = 1024
HALF = 512
GROUP = 8
TILE = 512
TILES = 8
MESH = pl.DeviceIdType.MESH
NT = (((1,), (1,)), ((), ()))
TN = (((0,), (0,)), ((), ()))

GATHER = ("p0a", "p0b", "m0a", "m0b", "y0a", "y0b", "p1a", "m1b", "p2a", "p2b", "m2a", "m2b", "y2a", "y2b")
SCATTER = ("p2q", "m2q", "p1k", "p1v", "m1k", "m1v", "p2", "m2", "y3", "p3k", "p3v", "m3k", "m3v")
PER_HEAD = len(GATHER) + len(SCATTER)
TP_SEM = 2 * PER_HEAD
PP_SEM = TP_SEM + TILES
HOP1_SEM = PP_SEM + TILES
HOP2_SEM = HOP1_SEM + 2
HOP3_SEM = HOP2_SEM + 2
RELAY_SEM = HOP3_SEM + 2
PASS_SEM = RELAY_SEM + 3
REMOTE_SEMS = PASS_SEM + 3
LONG_TILES = (1, 3)
RELAY_TILES = (0, 2, 4)
DIRECT_TILES = (5, 6, 7)
HID_SEM, Q_SEM, G_SEM, W_SEM = 0, 8, 9, 10
LOCAL_SEMS = 14


def kernel(
    hidden_ref, query_ref, grad_ref, kw_ref, vw_ref, len_ref,
    dq_ref, lg_ref, wk_ref, wv_ref,
    hid, qs, gs, wg, kv, acc, bias, gacc, gkv, gkvt, prod,
    rp2q, rm2q, rp1, rm1, rp2, rm2, ry3, rp3, rm3,
    lgs, lgr, lgo, hop1, hop2, held, ssem, rsem, lsem,
):
    dp, pp, tp = lax.axis_index("dp"), lax.axis_index("pp"), lax.axis_index("tp")
    x, y = dp // 2, dp % 2
    xp, xm, x2, yq = (x + 1) % 4, (x + 3) % 4, (x + 2) % 4, 1 - y
    j_me, j_p, j_m, j_2 = dp, xp * 2 + y, xm * 2 + y, x2 * 2 + y
    j_q, j_pq, j_mq, j_2q = x * 2 + yq, xp * 2 + yq, xm * 2 + yq, x2 * 2 + yq
    dev_p, dev_m, dev_y = (j_p, pp, tp), (j_m, pp, tp), (j_q, pp, tp)
    dev_t = (dp, pp, 1 - tp)
    hi, z = pp // 4, pp % 4
    z_up, z_down = (z + 1) % 4, (z + 3) % 4
    dev_prev = (dp, (pp + 7) % 8, tp)
    dev_up, dev_down = (dp, hi * 4 + z_up, tp), (dp, hi * 4 + z_down, tp)
    dev_far = (dp, (1 - hi) * 4 + z, tp)
    dev_far_up, dev_far_down = (dp, (1 - hi) * 4 + z_up, tp), (dp, (1 - hi) * 4 + z_down, tp)
    dev_hop3 = (dp, jnp.where(z == 2, 1 - hi, hi) * 4 + z_up, tp)

    sent = []

    def remote(src, dst, k, dev, arrival=None):
        return pltpu.make_async_remote_copy(
            src_ref=src, dst_ref=dst, send_sem=ssem.at[k], recv_sem=rsem.at[k if arrival is None else arrival],
            device_id=dev, device_id_type=MESH,
        )

    def local(src, dst, k):
        return pltpu.make_async_copy(src, dst, lsem.at[k])

    w_copies = []
    for h in range(2):
        for n, ref in enumerate((kw_ref, vw_ref)):
            c = local(ref.at[:, pl.ds(h * HD, HD)], wg.at[h, j_me, :, pl.ds(n * HD, HD)], W_SEM + 2 * h + n)
            c.start()
            w_copies.append(c)
    hid_copies = []
    for j in range(8):
        c = local(hidden_ref.at[:, pl.ds(j * SHARD, SHARD)], hid.at[:, pl.ds(j * SHARD, SHARD)], HID_SEM + j)
        c.start()
        hid_copies.append(c)
    q_copy = local(query_ref, qs, Q_SEM)
    g_copy = local(grad_ref, gs, G_SEM)
    q_copy.start()
    g_copy.start()

    barrier = pltpu.get_barrier_semaphore()
    for dev in (dev_p, dev_m, dev_y, dev_t, dev_up, dev_down, dev_far, dev_far_up, dev_far_down):
        pl.semaphore_signal(barrier, inc=1, device_id=dev, device_id_type=MESH)
    pl.semaphore_wait(barrier, 9)

    def gather_copy(h, name):
        dev = {"p": dev_p, "m": dev_m, "y": dev_y}[name[0]]
        j = {"p0": j_me, "m0": j_me, "y0": j_me, "p1": j_m, "m1": j_p, "p2": j_q, "m2": j_q, "y2": j_2}[name[:2]]
        rows = pl.ds(0 if name[2] == "a" else HALF, HALF)
        block = wg.at[h, j, rows]
        return remote(block, block, h * PER_HEAD + GATHER.index(name), dev)

    def gather_start(h, *names):
        for name in names:
            c = gather_copy(h, name)
            c.start()
            sent.append(c)

    def gather_wait(h, *names):
        for name in names:
            gather_copy(h, name).wait_recv()

    def project(h, j, first=False):
        columns = pl.ds(pl.multiple_of(j * SHARD, SHARD), SHARD)
        term = jnp.dot(hid[:, columns], wg[h, j], preferred_element_type=jnp.float32)
        if first:
            acc[...] = term
        else:
            acc[...] += term

    def project_half(h, j, half):
        columns = pl.ds(pl.multiple_of(j * SHARD + half * HALF, HALF), HALF)
        block = wg[h, j, pl.ds(half * HALF, HALF)]
        acc[...] += jnp.dot(hid[:, columns], block, preferred_element_type=jnp.float32)

    def attend(h, b):
        w0 = 128 * max(b - 1, 0)
        window = pl.ds(w0, 256)

        def pair(i, carry):
            c0 = pl.multiple_of((h * GROUP + 2 * i) * HD, 2 * HD)
            rows = pl.ds(b * 128, 128)
            q2 = jnp.concatenate([qs[rows, pl.ds(c0, HD)], qs[rows, pl.ds(c0 + HD, HD)]], axis=0)
            g2 = jnp.concatenate([gs[rows, pl.ds(c0, HD)], gs[rows, pl.ds(c0 + HD, HD)]], axis=0)
            keys = kv[h, window, pl.ds(0, HD)]
            values = kv[h, window, pl.ds(HD, HD)]
            mask = bias[b]
            s = lax.dot_general(keys, q2, NT, preferred_element_type=jnp.float32)
            s = s * (HD ** -0.5) + jnp.concatenate([mask, mask], axis=1)
            top = jnp.max(s, axis=0, keepdims=True)
            e = jnp.exp(s - top)
            p = e * (1.0 / jnp.sum(e, axis=0, keepdims=True))
            low = p.astype(jnp.bfloat16)
            dpr = lax.dot_general(values, g2, NT, preferred_element_type=jnp.float32)
            delta = jnp.sum(low.astype(jnp.float32) * dpr, axis=0, keepdims=True)
            ds = (p * (dpr - delta)).astype(jnp.bfloat16)
            dq = lax.dot_general(ds, keys, TN, preferred_element_type=jnp.float32) * (HD ** -0.5)
            dq = dq.astype(jnp.bfloat16)
            dq_ref[rows, pl.ds(c0, HD)] = dq[:128]
            dq_ref[rows, pl.ds(c0 + HD, HD)] = dq[128:]
            gacc[window, pl.ds(0, HD)] += jnp.dot(ds, q2, preferred_element_type=jnp.float32)
            gacc[window, pl.ds(HD, HD)] += jnp.dot(low, g2, preferred_element_type=jnp.float32)
            return carry

        lax.fori_loop(0, GROUP // 2, pair, 0, unroll=4)

    def finish_head(h):
        columns = pl.ds(h * GROUP * HD, GROUP * HD)
        key_part = gacc[:, pl.ds(0, HD)] * (HD ** -0.5)
        value_part = gacc[:, pl.ds(HD, HD)]
        gkv[h, :, pl.ds(0, HD)] = key_part.astype(jnp.bfloat16)
        gkv[h, :, pl.ds(HD, HD)] = value_part.astype(jnp.bfloat16)

    def flip_head(h):
        gkvt[h, pl.ds(0, HD), :] = (gacc[:, pl.ds(0, HD)] * (HD ** -0.5)).T.astype(jnp.bfloat16)
        gkvt[h, pl.ds(HD, HD), :] = gacc[:, pl.ds(HD, HD)].T.astype(jnp.bfloat16)

    targets = (j_2q, j_pq, j_mq, j_2, j_q, j_p, j_m)

    def term(h, j):
        columns = pl.ds(pl.multiple_of(j * SHARD, SHARD), SHARD)
        out = jnp.dot(gkvt[h], hid[:, columns], preferred_element_type=jnp.float32)
        return (out * ((ROWS * 8) ** -0.5)).astype(jnp.bfloat16)

    def terms(h, *slots):
        for n in slots:
            prod[h, n] = term(h, targets[n])

    krows, vrows = pl.ds(0, HD), pl.ds(HD, HD)

    def scatter_copy(h, name):
        src, dst, dev = {
            "p2q": (prod.at[h, 0, krows], rp2q.at[h], dev_p),
            "m2q": (prod.at[h, 0, vrows], rm2q.at[h], dev_m),
            "p1k": (prod.at[h, 1, krows], rp1.at[h, krows], dev_p),
            "p1v": (prod.at[h, 1, vrows], rp1.at[h, vrows], dev_p),
            "m1k": (prod.at[h, 2, krows], rm1.at[h, krows], dev_m),
            "m1v": (prod.at[h, 2, vrows], rm1.at[h, vrows], dev_m),
            "p2": (prod.at[h, 3, krows], rp2.at[h], dev_p),
            "m2": (prod.at[h, 3, vrows], rm2.at[h], dev_m),
            "y3": (prod.at[h, 4], ry3.at[h], dev_y),
            "p3k": (prod.at[h, 5, krows], rp3.at[h, krows], dev_p),
            "p3v": (prod.at[h, 5, vrows], rp3.at[h, vrows], dev_p),
            "m3k": (prod.at[h, 6, krows], rm3.at[h, krows], dev_m),
            "m3v": (prod.at[h, 6, vrows], rm3.at[h, vrows], dev_m),
        }[name]
        return remote(src, dst, h * PER_HEAD + len(GATHER) + SCATTER.index(name), dev)

    def scatter_start(h, *names):
        for name in names:
            c = scatter_copy(h, name)
            c.start()
            sent.append(c)

    def scatter_wait(h, *names):
        for name in names:
            scatter_copy(h, name).wait_recv()

    def wide(block):
        return block.astype(jnp.float32)

    def add(h, n, rows, *arrived):
        total = wide(prod[h, n, rows])
        for block in arrived:
            total = total + wide(block)
        prod[h, n, rows] = total.astype(jnp.bfloat16)

    def scatter_first(h):
        scatter_start(h, "p2q", "m2q", "p1v", "m1k", "p2", "m2")

    def scatter_second(h):
        scatter_wait(h, "p2q", "m2q")
        add(h, 1, krows, rp2q[h])
        scatter_start(h, "p1k")
        add(h, 2, vrows, rm2q[h])
        scatter_start(h, "m1v")
        scatter_wait(h, "p2", "m2")
        add(h, 5, krows, rp2[h])
        scatter_start(h, "p3k")
        add(h, 6, vrows, rm2[h])
        scatter_start(h, "m3v")

    def scatter_third(h):
        scatter_wait(h, "p1k", "p1v", "m1k", "m1v")
        add(h, 4, krows, rp1[h, krows], rm1[h, krows])
        add(h, 4, vrows, rp1[h, vrows], rm1[h, vrows])
        scatter_start(h, "y3")

    def scatter_last(h):
        own = term(h, j_me)
        scatter_wait(h, "y3", "p3k", "p3v", "m3k", "m3v")
        total = wide(own) + wide(ry3[h]) + wide(rp3[h]) + wide(rm3[h])
        wk_ref[:, pl.ds(h * HD, HD)] = total[:HD].T
        wv_ref[:, pl.ds(h * HD, HD)] = total[HD:].T

    for c in w_copies[:2]:
        c.wait()
    gather_start(0, "p0a", "m0b", "y0a", "p0b", "m0a", "y0b")
    for c in w_copies[2:]:
        c.wait()
    ends, last = [], jnp.int32(0)
    for k in range(8):
        last = last + len_ref[0, k]
        ends.append(last)
    for b in range(4):
        w0 = 128 * max(b - 1, 0)
        key_at = lax.broadcasted_iota(jnp.int32, (256, 128), 0) + w0
        query_at = lax.broadcasted_iota(jnp.int32, (256, 128), 1) + b * 128
        key_doc = jnp.zeros((256, 128), jnp.int32)
        query_doc = jnp.zeros((256, 128), jnp.int32)
        for end in ends:
            key_doc += (key_at >= end).astype(jnp.int32)
            query_doc += (query_at >= end).astype(jnp.int32)
        bias[b] = jnp.where((key_doc == query_doc) & (key_at <= query_at), 0.0, -1e30)
    for c in hid_copies:
        c.wait()
    project(0, j_me, True)
    gather_wait(0, "p0a", "m0b")
    gather_start(0, "p1a", "m1b")
    gather_wait(0, "y0a")
    gather_start(0, "p2a", "m2a")
    gather_wait(0, "m0a")
    gather_wait(0, "p0b", "y0b")
    gather_start(0, "p2b", "m2b")
    for j in (j_m, j_p, j_q):
        project(0, j)
    gather_wait(0, "p1a")
    gather_start(0, "y2a")
    gather_wait(0, "m1b")
    gather_start(0, "y2b")
    project(0, j_2)
    gather_wait(0, "p2a", "m2a")
    gather_start(1, "p0a", "m0b", "p0b", "m0a")
    gather_wait(0, "y2a")
    gather_start(1, "y0a", "y0b")
    gather_wait(0, "p2b", "m2b")
    project(0, j_pq)
    project(0, j_mq)
    gather_wait(0, "y2b")
    project(0, j_2q)
    kv[0] = acc[...].astype(jnp.bfloat16)
    q_copy.wait()
    g_copy.wait()

    gacc[...] = jnp.zeros_like(gacc)
    attend(0, 0)
    gather_wait(1, "p0a", "m0b")
    gather_start(1, "p1a", "m1b")
    gather_wait(1, "y0a")
    gather_start(1, "p2a", "m2a")
    attend(0, 1)
    gather_wait(1, "m0a")
    gather_wait(1, "p0b", "y0b")
    gather_start(1, "p2b", "m2b")
    attend(0, 2)
    gather_wait(1, "p1a")
    gather_start(1, "y2a")
    gather_wait(1, "m1b")
    gather_start(1, "y2b")
    attend(0, 3)
    finish_head(0)
    flip_head(0)
    terms(0, 0, 1, 2, 3)
    project(1, j_me, True)
    for j in (j_m, j_p, j_q, j_2):
        project(1, j)
    terms(0, 4, 5, 6)
    gather_wait(1, "p2a", "m2a", "y2a")
    scatter_first(0)
    scatter_start(0, "p3v", "m3k")
    project_half(1, j_pq, 0)
    project_half(1, j_mq, 0)
    project_half(1, j_2q, 0)
    gather_wait(1, "p2b", "m2b")
    project_half(1, j_pq, 1)
    project_half(1, j_mq, 1)
    gather_wait(1, "y2b")
    project_half(1, j_2q, 1)
    kv[1] = acc[...].astype(jnp.bfloat16)

    gacc[...] = jnp.zeros_like(gacc)
    attend(1, 0)
    attend(1, 1)
    attend(1, 2)
    attend(1, 3)
    finish_head(1)

    def tp_copy(t):
        return remote(lgs.at[t % 2], lgr.at[t], TP_SEM + t, dev_t)

    def out_tile(t):
        return lg_ref.at[:, pl.ds(pl.multiple_of(t * TILE, TILE), TILE)]

    def pp_copy(t):
        return remote(lgo.at[t], out_tile(t), PP_SEM + t, dev_prev)

    def relay_copy(i, t):
        return remote(lgo.at[t], held.at[i], RELAY_SEM + i, dev_down)

    def pass_copy(i, t):
        return remote(held.at[i], out_tile(t), PASS_SEM + i, dev_far, PP_SEM + t)

    def hop1_copy(i, t):
        return remote(lgo.at[t], hop1.at[i], HOP1_SEM + i, dev_up)

    def hop2_copy(i):
        return remote(hop1.at[i], hop2.at[i], HOP2_SEM + i, dev_up)

    def hop3_copy(i, t):
        return remote(hop2.at[i], out_tile(t), HOP3_SEM + i, dev_hop3, PP_SEM + t)

    def second_hop(i):
        hop1_copy(i, LONG_TILES[i]).wait_recv()
        hop2_copy(i).start()

    def third_hop(i):
        hop2_copy(i).wait_recv()
        hop3_copy(i, LONG_TILES[i]).start()

    def pass_on(i):
        @pl.when(z == 3)
        def _():
            relay_copy(i, RELAY_TILES[i]).wait_recv()
            pass_copy(i, RELAY_TILES[i]).start()

    def send_tile(t):
        is_long = (t == LONG_TILES[0]) | (t == LONG_TILES[1])
        is_relay = (z == 0) & ((t == RELAY_TILES[0]) | (t == RELAY_TILES[1]) | (t == RELAY_TILES[2]))

        @pl.when(is_long)
        def _():
            hop1_copy(t // 2, t).start()

        @pl.when(is_relay)
        def _():
            relay_copy(t // 2, t).start()

        @pl.when(jnp.logical_not(is_long) & ((z != 0) | (t == DIRECT_TILES[0])))
        def _():
            pp_copy(t).start()

    def layer_tile(half, t):
        j = half * 4 + t // 2
        rows = pl.ds(pl.multiple_of((t % 2) * TILE, TILE), TILE)
        return lax.dot_general(gkv[0], wg[0, j, rows], NT, preferred_element_type=jnp.float32) + lax.dot_general(
            gkv[1], wg[1, j, rows], NT, preferred_element_type=jnp.float32
        )

    def layer_step(t, carry):
        @pl.when((t >= 2) & (t < TILES))
        def _():
            tp_copy(t - 2).wait_send()

        @pl.when(t < TILES)
        def _():
            lgs[t % 2] = layer_tile(1 - tp, t).astype(jnp.bfloat16)
            tp_copy(t).start()
            lgo[t] = layer_tile(tp, t).astype(jnp.bfloat16)

        @pl.when(t > 0)
        def _():
            tp_copy(t - 1).wait_recv()
            lgo[t - 1] = (wide(lgo[t - 1]) + wide(lgr[t - 1])).astype(jnp.bfloat16)
            send_tile(t - 1)

        return carry

    lax.fori_loop(0, TILES + 1, layer_step, 0)

    def release(t, wait):
        @pl.when(z == 0)
        def _():
            if wait:
                relay_copy(1, RELAY_TILES[1]).wait_send()
            pp_copy(t).start()

    scatter_second(0)
    flip_head(1)
    terms(1, 0, 1, 2, 3)
    scatter_first(1)
    terms(1, 4, 5, 6)
    scatter_start(1, "p3v", "m3k")
    second_hop(0)
    scatter_third(0)
    pass_on(0)
    second_hop(1)
    scatter_last(0)
    scatter_second(1)
    release(DIRECT_TILES[1], True)
    pass_on(1)
    third_hop(0)
    scatter_third(1)
    release(DIRECT_TILES[2], False)
    third_hop(1)
    pass_on(2)
    scatter_last(1)
    for c in sent:
        c.wait_send()
    for t in range(TILES - 2, TILES):
        tp_copy(t).wait_send()
    for i, t in enumerate(LONG_TILES):
        hop1_copy(i, t).wait_send()
        hop2_copy(i).wait_send()
        hop3_copy(i, t).wait_send()
    for t in range(TILES):
        if t in LONG_TILES:
            continue
        if t not in RELAY_TILES:
            pp_copy(t).wait_send()
            continue
        i = RELAY_TILES.index(t)

        @pl.when(z == 0)
        def _(i=i, t=t):
            if i != 1:
                relay_copy(i, t).wait_send()

        @pl.when(z != 0)
        def _(t=t):
            pp_copy(t).wait_send()

        @pl.when(z == 3)
        def _(i=i, t=t):
            pass_copy(i, t).wait_send()

    for t in range(TILES):
        pp_copy(t).wait_recv()


def body(hidden_in, queries, out_grad, key_weight, value_weight, doc_lengths):
    any_space = pl.BlockSpec(memory_space=pl.ANY)
    vmem_space = pl.BlockSpec(memory_space=pltpu.VMEM)
    bf16, f32 = jnp.bfloat16, jnp.float32
    block = (2, 2 * HD, SHARD)
    outs = pl.pallas_call(
        kernel,
        out_shape=(
            pltpu.VMEM((ROWS, 2048), bf16),
            pltpu.VMEM((ROWS, WIDTH // 2), bf16),
            pltpu.VMEM((SHARD, 2 * HD), f32),
            pltpu.VMEM((SHARD, 2 * HD), f32),
        ),
        in_specs=[any_space] * 5 + [pl.BlockSpec(memory_space=pltpu.SMEM)],
        out_specs=(vmem_space,) * 4,
        scratch_shapes=[
            pltpu.VMEM((ROWS, WIDTH), bf16),
            pltpu.VMEM((ROWS, 2048), bf16),
            pltpu.VMEM((ROWS, 2048), bf16),
            pltpu.VMEM((2, 8, SHARD, 2 * HD), bf16),
            pltpu.VMEM((2, ROWS, 2 * HD), bf16),
            pltpu.VMEM((ROWS, 2 * HD), f32),
            pltpu.VMEM((4, 256, 128), f32),
            pltpu.VMEM((ROWS, 2 * HD), f32),
            pltpu.VMEM((2, ROWS, 2 * HD), bf16),
            pltpu.VMEM((2, 2 * HD, ROWS), bf16),
            pltpu.VMEM((2, 7, 2 * HD, SHARD), bf16),
            pltpu.VMEM((2, HD, SHARD), bf16),
            pltpu.VMEM((2, HD, SHARD), bf16),
            pltpu.VMEM(block, bf16),
            pltpu.VMEM(block, bf16),
            pltpu.VMEM((2, HD, SHARD), bf16),
            pltpu.VMEM((2, HD, SHARD), bf16),
            pltpu.VMEM(block, bf16),
            pltpu.VMEM(block, bf16),
            pltpu.VMEM(block, bf16),
            pltpu.VMEM((2, ROWS, TILE), bf16),
            pltpu.VMEM((TILES, ROWS, TILE), bf16),
            pltpu.VMEM((TILES, ROWS, TILE), bf16),
            pltpu.VMEM((2, ROWS, TILE), bf16),
            pltpu.VMEM((2, ROWS, TILE), bf16),
            pltpu.VMEM((3, ROWS, TILE), bf16),
            pltpu.SemaphoreType.DMA((REMOTE_SEMS,)),
            pltpu.SemaphoreType.DMA((REMOTE_SEMS,)),
            pltpu.SemaphoreType.DMA((LOCAL_SEMS,)),
        ],
        compiler_params=pltpu.CompilerParams(
            collective_id=0, has_side_effects=True, vmem_limit_bytes=53 * 1024 * 1024
        ),
        cost_estimate=pl.CostEstimate(flops=18_000_000_000, bytes_accessed=24_000_000, transcendentals=2_100_000),
    )(hidden_in[0], queries[0], out_grad[0], key_weight[0], value_weight[0], doc_lengths[0])
    return tuple(out[None] for out in outs)


def solution(mesh):
    return jax.shard_map(
        body,
        mesh=mesh,
        in_specs=(
            P("pp", "dp", None),
            P("pp", "dp", "tp"),
            P("pp", "dp", "tp"),
            P("pp", "dp", "tp"),
            P("pp", "dp", "tp"),
            P("pp", "dp", None),
        ),
        out_specs=(
            P("pp", "dp", "tp"),
            P("pp", "dp", "tp"),
            P("pp", "dp", "tp"),
            P("pp", "dp", "tp"),
        ),
        check_vma=False,
    )
```

```python
import functools

import jax
import jax.numpy as jnp
from jax import lax
from jax.experimental import pallas as pl
from jax.experimental.pallas import tpu as pltpu
from jax.sharding import PartitionSpec as P

HD = 128
ROWS = 512
WIDTH = 8192
SHARD = 1024
HALF = 512
GROUP = 8
TILE = 512
TILES = 8
MESH = pl.DeviceIdType.MESH
NT = (((1,), (1,)), ((), ()))
TN = (((0,), (0,)), ((), ()))

GATHER = ("p0a", "p0b", "m0a", "m0b", "y0a", "y0b", "p1a", "m1b", "p2a", "p2b", "m2a", "m2b", "y2a", "y2b")
SCATTER = ("p2q", "m2q", "p1k", "p1v", "m1k", "m1v", "p2", "m2", "y3", "p3k", "p3v", "m3k", "m3v")
PER_HEAD = len(GATHER) + len(SCATTER)
TP_SEM = 2 * PER_HEAD
PP_SEM = TP_SEM + TILES
HOP1_SEM = PP_SEM + TILES
HOP2_SEM = HOP1_SEM + 2
HOP3_SEM = HOP2_SEM + 2
RELAY_SEM = HOP3_SEM + 2
PASS_SEM = RELAY_SEM + 3
TAIL_SEM = PASS_SEM + 3
TAIL_PASS_SEM = TAIL_SEM + 1
REMOTE_SEMS = TAIL_PASS_SEM + 1
LONG_TILES = (1, 3)
RELAY_TILES = (0, 2, 4)
DIRECT_TILES = (5, 6, 7)
HID_SEM, Q_SEM, G_SEM, W_SEM = 0, 8, 9, 10
LOCAL_SEMS = 14


def kernel(
    hidden_ref, query_ref, grad_ref, kw_ref, vw_ref, len_ref,
    dq_ref, lg_ref, wk_ref, wv_ref,
    hid, qs, gs, wg, kv, acc, bias, gacc, gkv, gkvt, prod,
    rp2q, rm2q, rp1, rm1, rp2, rm2, ry3, rp3, rm3,
    lgs, lgr, lgo, hop1, hop2, held, ssem, rsem, lsem,
):
    dp, pp, tp = lax.axis_index("dp"), lax.axis_index("pp"), lax.axis_index("tp")
    x, y = dp // 2, dp % 2
    xp, xm, x2, yq = (x + 1) % 4, (x + 3) % 4, (x + 2) % 4, 1 - y
    j_me, j_p, j_m, j_2 = dp, xp * 2 + y, xm * 2 + y, x2 * 2 + y
    j_q, j_pq, j_mq, j_2q = x * 2 + yq, xp * 2 + yq, xm * 2 + yq, x2 * 2 + yq
    dev_p, dev_m, dev_y = (j_p, pp, tp), (j_m, pp, tp), (j_q, pp, tp)
    dev_t = (dp, pp, 1 - tp)
    hi, z = pp // 4, pp % 4
    z_up, z_down = (z + 1) % 4, (z + 3) % 4
    dev_prev = (dp, (pp + 7) % 8, tp)
    dev_up, dev_down = (dp, hi * 4 + z_up, tp), (dp, hi * 4 + z_down, tp)
    dev_far = (dp, (1 - hi) * 4 + z, tp)
    dev_far_up, dev_far_down = (dp, (1 - hi) * 4 + z_up, tp), (dp, (1 - hi) * 4 + z_down, tp)
    dev_hop3 = (dp, jnp.where(z == 2, 1 - hi, hi) * 4 + z_up, tp)

    sent = []

    def remote(src, dst, k, dev, arrival=None):
        return pltpu.make_async_remote_copy(
            src_ref=src, dst_ref=dst, send_sem=ssem.at[k], recv_sem=rsem.at[k if arrival is None else arrival],
            device_id=dev, device_id_type=MESH,
        )

    def local(src, dst, k):
        return pltpu.make_async_copy(src, dst, lsem.at[k])

    w_copies = []
    for h in range(2):
        for n, ref in enumerate((kw_ref, vw_ref)):
            c = local(ref.at[:, pl.ds(h * HD, HD)], wg.at[h, j_me, :, pl.ds(n * HD, HD)], W_SEM + 2 * h + n)
            c.start()
            w_copies.append(c)
    hid_copies = []
    for j in range(8):
        c = local(hidden_ref.at[:, pl.ds(j * SHARD, SHARD)], hid.at[:, pl.ds(j * SHARD, SHARD)], HID_SEM + j)
        c.start()
        hid_copies.append(c)
    q_copy = local(query_ref, qs, Q_SEM)
    g_copy = local(grad_ref, gs, G_SEM)
    q_copy.start()
    g_copy.start()

    barrier = pltpu.get_barrier_semaphore()
    for dev in (dev_p, dev_m, dev_y, dev_t, dev_up, dev_down, dev_far, dev_far_up, dev_far_down):
        pl.semaphore_signal(barrier, inc=1, device_id=dev, device_id_type=MESH)
    pl.semaphore_wait(barrier, 9)

    def gather_copy(h, name):
        dev = {"p": dev_p, "m": dev_m, "y": dev_y}[name[0]]
        j = {"p0": j_me, "m0": j_me, "y0": j_me, "p1": j_m, "m1": j_p, "p2": j_q, "m2": j_q, "y2": j_2}[name[:2]]
        rows = pl.ds(0 if name[2] == "a" else HALF, HALF)
        block = wg.at[h, j, rows]
        return remote(block, block, h * PER_HEAD + GATHER.index(name), dev)

    def gather_start(h, *names):
        for name in names:
            c = gather_copy(h, name)
            c.start()
            sent.append(c)

    def gather_wait(h, *names):
        for name in names:
            gather_copy(h, name).wait_recv()

    def project(h, j, first=False):
        columns = pl.ds(pl.multiple_of(j * SHARD, SHARD), SHARD)
        term = jnp.dot(hid[:, columns], wg[h, j], preferred_element_type=jnp.float32)
        if first:
            acc[...] = term
        else:
            acc[...] += term

    def project_half(h, j, half):
        columns = pl.ds(pl.multiple_of(j * SHARD + half * HALF, HALF), HALF)
        block = wg[h, j, pl.ds(half * HALF, HALF)]
        acc[...] += jnp.dot(hid[:, columns], block, preferred_element_type=jnp.float32)

    def attend(h, b):
        w0 = 128 * max(b - 1, 0)
        window = pl.ds(w0, 256)

        def pair(i, carry):
            c0 = pl.multiple_of((h * GROUP + 2 * i) * HD, 2 * HD)
            rows = pl.ds(b * 128, 128)
            q2 = jnp.concatenate([qs[rows, pl.ds(c0, HD)], qs[rows, pl.ds(c0 + HD, HD)]], axis=0)
            g2 = jnp.concatenate([gs[rows, pl.ds(c0, HD)], gs[rows, pl.ds(c0 + HD, HD)]], axis=0)
            keys = kv[h, window, pl.ds(0, HD)]
            values = kv[h, window, pl.ds(HD, HD)]
            mask = bias[b]
            s = lax.dot_general(keys, q2, NT, preferred_element_type=jnp.float32)
            s = s * (HD ** -0.5) + jnp.concatenate([mask, mask], axis=1)
            top = jnp.max(s, axis=0, keepdims=True)
            e = jnp.exp(s - top)
            p = e * (1.0 / jnp.sum(e, axis=0, keepdims=True))
            low = p.astype(jnp.bfloat16)
            dpr = lax.dot_general(values, g2, NT, preferred_element_type=jnp.float32)
            delta = jnp.sum(low.astype(jnp.float32) * dpr, axis=0, keepdims=True)
            ds = (p * (dpr - delta)).astype(jnp.bfloat16)
            dq = lax.dot_general(ds, keys, TN, preferred_element_type=jnp.float32) * (HD ** -0.5)
            dq = dq.astype(jnp.bfloat16)
            dq_ref[rows, pl.ds(c0, HD)] = dq[:128]
            dq_ref[rows, pl.ds(c0 + HD, HD)] = dq[128:]
            gacc[window, pl.ds(0, HD)] += jnp.dot(ds, q2, preferred_element_type=jnp.float32)
            gacc[window, pl.ds(HD, HD)] += jnp.dot(low, g2, preferred_element_type=jnp.float32)
            return carry

        lax.fori_loop(0, GROUP // 2, pair, 0, unroll=4)

    def finish_head(h):
        columns = pl.ds(h * GROUP * HD, GROUP * HD)
        key_part = gacc[:, pl.ds(0, HD)] * (HD ** -0.5)
        value_part = gacc[:, pl.ds(HD, HD)]
        gkv[h, :, pl.ds(0, HD)] = key_part.astype(jnp.bfloat16)
        gkv[h, :, pl.ds(HD, HD)] = value_part.astype(jnp.bfloat16)

    def flip_head(h):
        gkvt[h, pl.ds(0, HD), :] = (gacc[:, pl.ds(0, HD)] * (HD ** -0.5)).T.astype(jnp.bfloat16)
        gkvt[h, pl.ds(HD, HD), :] = gacc[:, pl.ds(HD, HD)].T.astype(jnp.bfloat16)

    targets = (j_2q, j_pq, j_mq, j_2, j_q, j_p, j_m)

    def term(h, j):
        columns = pl.ds(pl.multiple_of(j * SHARD, SHARD), SHARD)
        out = jnp.dot(gkvt[h], hid[:, columns], preferred_element_type=jnp.float32)
        return (out * ((ROWS * 8) ** -0.5)).astype(jnp.bfloat16)

    def terms(h, *slots):
        for n in slots:
            prod[h, n] = term(h, targets[n])

    krows, vrows = pl.ds(0, HD), pl.ds(HD, HD)

    def scatter_copy(h, name):
        src, dst, dev = {
            "p2q": (prod.at[h, 0, krows], rp2q.at[h], dev_p),
            "m2q": (prod.at[h, 0, vrows], rm2q.at[h], dev_m),
            "p1k": (prod.at[h, 1, krows], rp1.at[h, krows], dev_p),
            "p1v": (prod.at[h, 1, vrows], rp1.at[h, vrows], dev_p),
            "m1k": (prod.at[h, 2, krows], rm1.at[h, krows], dev_m),
            "m1v": (prod.at[h, 2, vrows], rm1.at[h, vrows], dev_m),
            "p2": (prod.at[h, 3, krows], rp2.at[h], dev_p),
            "m2": (prod.at[h, 3, vrows], rm2.at[h], dev_m),
            "y3": (prod.at[h, 4], ry3.at[h], dev_y),
            "p3k": (prod.at[h, 5, krows], rp3.at[h, krows], dev_p),
            "p3v": (prod.at[h, 5, vrows], rp3.at[h, vrows], dev_p),
            "m3k": (prod.at[h, 6, krows], rm3.at[h, krows], dev_m),
            "m3v": (prod.at[h, 6, vrows], rm3.at[h, vrows], dev_m),
        }[name]
        return remote(src, dst, h * PER_HEAD + len(GATHER) + SCATTER.index(name), dev)

    def scatter_start(h, *names):
        for name in names:
            c = scatter_copy(h, name)
            c.start()
            sent.append(c)

    def scatter_wait(h, *names):
        for name in names:
            scatter_copy(h, name).wait_recv()

    def wide(block):
        return block.astype(jnp.float32)

    def add(h, n, rows, *arrived):
        total = wide(prod[h, n, rows])
        for block in arrived:
            total = total + wide(block)
        prod[h, n, rows] = total.astype(jnp.bfloat16)

    def scatter_first(h):
        scatter_start(h, "p2q", "m2q", "p1v", "m1k", "p2", "m2")

    def scatter_second(h):
        scatter_wait(h, "p2q", "m2q")
        add(h, 1, krows, rp2q[h])
        scatter_start(h, "p1k")
        add(h, 2, vrows, rm2q[h])
        scatter_start(h, "m1v")
        scatter_wait(h, "p2", "m2")
        add(h, 5, krows, rp2[h])
        scatter_start(h, "p3k")
        add(h, 6, vrows, rm2[h])
        scatter_start(h, "m3v")

    def scatter_third(h):
        scatter_wait(h, "p1k", "p1v", "m1k", "m1v")
        add(h, 4, krows, rp1[h, krows], rm1[h, krows])
        add(h, 4, vrows, rp1[h, vrows], rm1[h, vrows])
        scatter_start(h, "y3")

    def scatter_last(h):
        own = term(h, j_me)
        scatter_wait(h, "y3", "p3k", "p3v", "m3k", "m3v")
        total = wide(own) + wide(ry3[h]) + wide(rp3[h]) + wide(rm3[h])
        wk_ref[:, pl.ds(h * HD, HD)] = total[:HD].T
        wv_ref[:, pl.ds(h * HD, HD)] = total[HD:].T

    for c in w_copies[:2]:
        c.wait()
    gather_start(0, "p0a", "m0b", "y0a", "p0b", "m0a", "y0b")
    for c in w_copies[2:]:
        c.wait()
    ends, last = [], jnp.int32(0)
    for k in range(8):
        last = last + len_ref[0, k]
        ends.append(last)
    for b in range(4):
        w0 = 128 * max(b - 1, 0)
        key_at = lax.broadcasted_iota(jnp.int32, (256, 128), 0) + w0
        query_at = lax.broadcasted_iota(jnp.int32, (256, 128), 1) + b * 128
        key_doc = jnp.zeros((256, 128), jnp.int32)
        query_doc = jnp.zeros((256, 128), jnp.int32)
        for end in ends:
            key_doc += (key_at >= end).astype(jnp.int32)
            query_doc += (query_at >= end).astype(jnp.int32)
        bias[b] = jnp.where((key_doc == query_doc) & (key_at <= query_at), 0.0, -1e30)
    for c in hid_copies:
        c.wait()
    project(0, j_me, True)
    gather_wait(0, "p0a", "m0b")
    gather_start(0, "p1a", "m1b")
    gather_wait(0, "y0a")
    gather_start(0, "p2a", "m2a")
    gather_wait(0, "m0a")
    gather_wait(0, "p0b", "y0b")
    gather_start(0, "p2b", "m2b")
    for j in (j_m, j_p, j_q):
        project(0, j)
    gather_wait(0, "p1a")
    gather_start(0, "y2a")
    gather_wait(0, "m1b")
    gather_start(0, "y2b")
    project(0, j_2)
    gather_wait(0, "p2a", "m2a")
    gather_start(1, "p0a", "m0b", "p0b", "m0a")
    gather_wait(0, "y2a")
    gather_start(1, "y0a", "y0b")
    gather_wait(0, "p2b", "m2b")
    project(0, j_pq)
    project(0, j_mq)
    gather_wait(0, "y2b")
    project(0, j_2q)
    kv[0] = acc[...].astype(jnp.bfloat16)
    q_copy.wait()
    g_copy.wait()

    gacc[...] = jnp.zeros_like(gacc)
    attend(0, 0)
    gather_wait(1, "p0a", "m0b")
    gather_start(1, "p1a", "m1b")
    gather_wait(1, "y0a")
    gather_start(1, "p2a", "m2a")
    attend(0, 1)
    gather_wait(1, "m0a")
    gather_wait(1, "p0b", "y0b")
    gather_start(1, "p2b", "m2b")
    attend(0, 2)
    gather_wait(1, "p1a")
    gather_start(1, "y2a")
    gather_wait(1, "m1b")
    gather_start(1, "y2b")
    attend(0, 3)
    finish_head(0)
    flip_head(0)
    terms(0, 0, 1, 2, 3)
    project(1, j_me, True)
    for j in (j_m, j_p, j_q, j_2):
        project(1, j)
    terms(0, 4, 5, 6)
    gather_wait(1, "p2a", "m2a", "y2a")
    scatter_first(0)
    scatter_start(0, "p3v", "m3k")
    project_half(1, j_pq, 0)
    project_half(1, j_mq, 0)
    project_half(1, j_2q, 0)
    gather_wait(1, "p2b", "m2b")
    project_half(1, j_pq, 1)
    project_half(1, j_mq, 1)
    gather_wait(1, "y2b")
    project_half(1, j_2q, 1)
    kv[1] = acc[...].astype(jnp.bfloat16)

    gacc[...] = jnp.zeros_like(gacc)
    attend(1, 0)
    attend(1, 1)
    attend(1, 2)
    attend(1, 3)
    finish_head(1)

    def tp_copy(t):
        return remote(lgs.at[t % 2], lgr.at[t], TP_SEM + t, dev_t)

    def out_tile(t):
        return lg_ref.at[:, pl.ds(pl.multiple_of(t * TILE, TILE), TILE)]

    def pp_copy(t):
        return remote(lgo.at[t], out_tile(t), PP_SEM + t, dev_prev)

    first_rows, tail_rows = pl.ds(0, ROWS // 2), pl.ds(ROWS // 2, ROWS // 2)
    tail_tile = RELAY_TILES[2]

    def out_rows(t, rows):
        return lg_ref.at[rows, pl.ds(t * TILE, TILE)]

    def relay_copy(i, t):
        return remote(lgo.at[t], held.at[i], RELAY_SEM + i, dev_down)

    def pass_copy(i, t):
        return remote(held.at[i], out_tile(t), PASS_SEM + i, dev_far, PP_SEM + t)

    def first_relay():
        return remote(lgo.at[tail_tile, first_rows], held.at[2, first_rows], RELAY_SEM + 2, dev_down)

    def tail_relay():
        return remote(lgo.at[tail_tile, tail_rows], held.at[2, tail_rows], TAIL_SEM, dev_down)

    def first_pass():
        return remote(held.at[2, first_rows], out_rows(tail_tile, first_rows), PASS_SEM + 2, dev_far, PP_SEM + tail_tile)

    def tail_pass():
        return remote(held.at[2, tail_rows], out_rows(tail_tile, tail_rows), TAIL_PASS_SEM, dev_far)

    def hop1_copy(i, t):
        return remote(lgo.at[t], hop1.at[i], HOP1_SEM + i, dev_up)

    def hop2_copy(i):
        return remote(hop1.at[i], hop2.at[i], HOP2_SEM + i, dev_up)

    def hop3_copy(i, t):
        return remote(hop2.at[i], out_tile(t), HOP3_SEM + i, dev_hop3, PP_SEM + t)

    def second_hop(i):
        hop1_copy(i, LONG_TILES[i]).wait_recv()
        hop2_copy(i).start()

    def third_hop(i):
        hop2_copy(i).wait_recv()
        hop3_copy(i, LONG_TILES[i]).start()

    def pass_on(i):
        @pl.when(z == 3)
        def _():
            if i == 2:
                first_relay().wait_recv()
                first_pass().start()
                tail_relay().wait_recv()
                tail_pass().start()
            else:
                relay_copy(i, RELAY_TILES[i]).wait_recv()
                pass_copy(i, RELAY_TILES[i]).start()

    def send_tile(t):
        is_long = (t == LONG_TILES[0]) | (t == LONG_TILES[1])
        is_relay = (z == 0) & ((t == RELAY_TILES[0]) | (t == RELAY_TILES[1]))

        @pl.when(is_long)
        def _():
            hop1_copy(t // 2, t).start()

        @pl.when(is_relay)
        def _():
            relay_copy(t // 2, t).start()

        is_tail = (z == 0) & (t == tail_tile)

        @pl.when(is_tail)
        def _():
            first_relay().start()
            tail_relay().start()

        @pl.when(jnp.logical_not(is_long) & ((z != 0) | (t == DIRECT_TILES[0])))
        def _():
            pp_copy(t).start()

    def layer_tile(half, t):
        j = half * 4 + t // 2
        rows = pl.ds(pl.multiple_of((t % 2) * TILE, TILE), TILE)
        return lax.dot_general(gkv[0], wg[0, j, rows], NT, preferred_element_type=jnp.float32) + lax.dot_general(
            gkv[1], wg[1, j, rows], NT, preferred_element_type=jnp.float32
        )

    def layer_step(t, carry):
        @pl.when((t >= 2) & (t < TILES))
        def _():
            tp_copy(t - 2).wait_send()

        @pl.when(t < TILES)
        def _():
            lgs[t % 2] = layer_tile(1 - tp, t).astype(jnp.bfloat16)
            tp_copy(t).start()
            lgo[t] = layer_tile(tp, t).astype(jnp.bfloat16)

        @pl.when(t > 0)
        def _():
            tp_copy(t - 1).wait_recv()
            lgo[t - 1] = (wide(lgo[t - 1]) + wide(lgr[t - 1])).astype(jnp.bfloat16)
            send_tile(t - 1)

        return carry

    lax.fori_loop(0, TILES + 1, layer_step, 0)

    def release(t, wait):
        @pl.when(z == 0)
        def _():
            if wait:
                relay_copy(1, RELAY_TILES[1]).wait_send()
            pp_copy(t).start()

    scatter_second(0)
    flip_head(1)
    terms(1, 0, 1, 2, 3)
    scatter_first(1)
    terms(1, 4, 5, 6)
    scatter_start(1, "p3v", "m3k")
    second_hop(0)
    scatter_third(0)
    pass_on(0)
    second_hop(1)
    scatter_last(0)
    scatter_second(1)
    release(DIRECT_TILES[1], True)
    pass_on(1)
    third_hop(0)
    scatter_third(1)
    release(DIRECT_TILES[2], False)
    third_hop(1)
    pass_on(2)
    scatter_last(1)
    for c in sent:
        c.wait_send()
    for t in range(TILES - 2, TILES):
        tp_copy(t).wait_send()
    for i, t in enumerate(LONG_TILES):
        hop1_copy(i, t).wait_send()
        hop2_copy(i).wait_send()
        hop3_copy(i, t).wait_send()
    for t in range(TILES):
        if t in LONG_TILES:
            continue
        if t not in RELAY_TILES:
            pp_copy(t).wait_send()
            continue
        i = RELAY_TILES.index(t)

        @pl.when(z == 0)
        def _(i=i, t=t):
            if i == 0:
                relay_copy(i, t).wait_send()
            if i == 2:
                first_relay().wait_send()
                tail_relay().wait_send()

        @pl.when(z != 0)
        def _(t=t):
            pp_copy(t).wait_send()

        @pl.when(z == 3)
        def _(i=i, t=t):
            if i == 2:
                first_pass().wait_send()
                tail_pass().wait_send()
            else:
                pass_copy(i, t).wait_send()

    @pl.when(z == 3)
    def _():
        first_pass().wait_recv()
        tail_pass().wait_recv()

    @pl.when(z != 3)
    def _():
        pp_copy(tail_tile).wait_recv()

    for t in range(TILES):
        if t != tail_tile:
            pp_copy(t).wait_recv()


def body(hidden_in, queries, out_grad, key_weight, value_weight, doc_lengths):
    any_space = pl.BlockSpec(memory_space=pl.ANY)
    vmem_space = pl.BlockSpec(memory_space=pltpu.VMEM)
    bf16, f32 = jnp.bfloat16, jnp.float32
    block = (2, 2 * HD, SHARD)
    outs = pl.pallas_call(
        kernel,
        out_shape=(
            pltpu.VMEM((ROWS, 2048), bf16),
            pltpu.VMEM((ROWS, WIDTH // 2), bf16),
            pltpu.VMEM((SHARD, 2 * HD), f32),
            pltpu.VMEM((SHARD, 2 * HD), f32),
        ),
        in_specs=[any_space] * 5 + [pl.BlockSpec(memory_space=pltpu.SMEM)],
        out_specs=(vmem_space,) * 4,
        scratch_shapes=[
            pltpu.VMEM((ROWS, WIDTH), bf16),
            pltpu.VMEM((ROWS, 2048), bf16),
            pltpu.VMEM((ROWS, 2048), bf16),
            pltpu.VMEM((2, 8, SHARD, 2 * HD), bf16),
            pltpu.VMEM((2, ROWS, 2 * HD), bf16),
            pltpu.VMEM((ROWS, 2 * HD), f32),
            pltpu.VMEM((4, 256, 128), f32),
            pltpu.VMEM((ROWS, 2 * HD), f32),
            pltpu.VMEM((2, ROWS, 2 * HD), bf16),
            pltpu.VMEM((2, 2 * HD, ROWS), bf16),
            pltpu.VMEM((2, 7, 2 * HD, SHARD), bf16),
            pltpu.VMEM((2, HD, SHARD), bf16),
            pltpu.VMEM((2, HD, SHARD), bf16),
            pltpu.VMEM(block, bf16),
            pltpu.VMEM(block, bf16),
            pltpu.VMEM((2, HD, SHARD), bf16),
            pltpu.VMEM((2, HD, SHARD), bf16),
            pltpu.VMEM(block, bf16),
            pltpu.VMEM(block, bf16),
            pltpu.VMEM(block, bf16),
            pltpu.VMEM((2, ROWS, TILE), bf16),
            pltpu.VMEM((TILES, ROWS, TILE), bf16),
            pltpu.VMEM((TILES, ROWS, TILE), bf16),
            pltpu.VMEM((2, ROWS, TILE), bf16),
            pltpu.VMEM((2, ROWS, TILE), bf16),
            pltpu.VMEM((3, ROWS, TILE), bf16),
            pltpu.SemaphoreType.DMA((REMOTE_SEMS,)),
            pltpu.SemaphoreType.DMA((REMOTE_SEMS,)),
            pltpu.SemaphoreType.DMA((LOCAL_SEMS,)),
        ],
        compiler_params=pltpu.CompilerParams(
            collective_id=0, has_side_effects=True, vmem_limit_bytes=53 * 1024 * 1024
        ),
        cost_estimate=pl.CostEstimate(flops=18_000_000_000, bytes_accessed=24_000_000, transcendentals=2_100_000),
    )(hidden_in[0], queries[0], out_grad[0], key_weight[0], value_weight[0], doc_lengths[0])
    return tuple(out[None] for out in outs)


def solution(mesh):
    return jax.shard_map(
        body,
        mesh=mesh,
        in_specs=(
            P("pp", "dp", None),
            P("pp", "dp", "tp"),
            P("pp", "dp", "tp"),
            P("pp", "dp", "tp"),
            P("pp", "dp", "tp"),
            P("pp", "dp", None),
        ),
        out_specs=(
            P("pp", "dp", "tp"),
            P("pp", "dp", "tp"),
            P("pp", "dp", "tp"),
            P("pp", "dp", "tp"),
        ),
        check_vma=False,
    )
```
